256 devices in a mesh: gx: 16 (over z_lo, y), gy: 16 (over z_hi, x, core).
Axes of the slice: x: 4, y: 4, z: 8 (z_hi: 2, z_lo: 4; z = z_hi * 4 + z_lo), core: 2. Of those that a mesh axis runs over, the one named last changes fastest.
Arguments:
- coarse_out: float32 [64, 64, 64, 128], P(None, 'gx', 'gy'), may hold values from -6 to 6
- coarse_cot: float32 [64, 64, 64, 128], P(None, 'gx', 'gy'), may hold values from -6 to 6
- fine_conv: float32 [27, 32, 8], replicated, may hold values from -0.4375 to 0.4375
- fine_bias_in: float32 [32], replicated, may hold values from -3 to 3
- fine_proj: float32 [16, 32], replicated, may hold values from -1 to 1
- fine_bias_out: float32 [16], replicated, may hold values from -3 to 3
- coarse_conv: float32 [27, 64, 32], replicated, may hold values from -0.21875 to 0.21875
- coarse_bias_in: float32 [64], replicated, may hold values from -3 to 3
- coarse_proj: float32 [64, 64], replicated, may hold values from -0.75 to 0.75
- coarse_bias_out: float32 [64], replicated, may hold values from -3 to 3
Outputs:
- input_field: float32 [16, 128, 128, 128], P(None, 'gx', 'gy')
- input_grad: float32 [16, 128, 128, 128], P(None, 'gx', 'gy')
- grad_fine_conv: float32 [27, 32, 8], replicated
- grad_fine_bias_in: float32 [32], replicated
- grad_fine_proj: float32 [16, 32], replicated
- grad_fine_bias_out: float32 [16], replicated
- grad_coarse_conv: float32 [27, 64, 32], replicated
- grad_coarse_bias_in: float32 [64], replicated
- grad_coarse_proj: float32 [64, 64], replicated
- grad_coarse_bias_out: float32 [64], replicated
The draws below stay inside these ranges and needn't reach their ends.
All inputs are finite; a program needn't handle non-finite values.
Results may differ from the reference program's by a relative error of at most 0.00021.
Values sent between devices are 32-bit elements; how exact they have to be, the bound alone decides.
No kernel may reach another device: no remote copies, remote signals or barrier semaphores. Data moves between devices by JAX's collectives and lax.ppermute only.
A program may use at most 128 MiB of HBM per device.

```python
import jax
import jax.numpy as jnp
from jax import lax

C = 16
HID1 = 32
HID2 = 64
NZ = 128
NX = 128
NY = 128


def block_levels(rng, extent, shards, smallest, top_value):
    loudness, own = 1.0, jax.random.fold_in(rng, 6)
    for dim, shards_of in shards:
        steps = jnp.exp(jax.random.uniform(jax.random.fold_in(own, dim), (shards_of,), jnp.float32, smallest / len(shards), top_value / len(shards)))
        loudness = loudness * jnp.repeat(steps, extent[dim] // shards_of).reshape([-1 if axis == dim else 1 for axis in range(len(extent))])
    return loudness


def noise(own_key, shape, spread, most, shards=(), held_as=jnp.bfloat16):
    result = jax.random.normal(own_key, shape, jnp.float32) * spread
    if len(shards) > 0:
        result = block_levels(own_key, shape, shards, -0.22, 0.18) * result
    return jnp.clip(result, min=-most, max=most).astype(held_as)


def setup_inputs(seed: int = 0) -> dict:
    arg_keys = jax.random.split(jax.random.key(seed), 11)
    coarse_out = noise(arg_keys[0], (4 * C, NX // 2, NY // 2, NZ), 1.0, 6.0, ((1, 16), (2, 16)), jnp.float32)
    coarse_cot = noise(arg_keys[1], (4 * C, NX // 2, NY // 2, NZ), 1.0, 6.0, ((1, 16), (2, 16)), jnp.float32)
    fine_conv = noise(arg_keys[2], (27, HID1, C // 2), (27 * C // 2) ** -0.5, 0.4375, (), jnp.float32)
    fine_bias_in = noise(arg_keys[3], (HID1,), 0.5, 3.0, (), jnp.float32)
    fine_proj = noise(arg_keys[4], (C, HID1), HID1 ** -0.5, 1.0, (), jnp.float32)
    fine_bias_out = noise(arg_keys[5], (C,), 0.5, 3.0, (), jnp.float32)
    coarse_conv = noise(arg_keys[6], (27, HID2, 2 * C), (54 * C) ** -0.5, 0.21875, (), jnp.float32)
    coarse_bias_in = noise(arg_keys[7], (HID2,), 0.5, 3.0, (), jnp.float32)
    coarse_proj = noise(arg_keys[8], (4 * C, HID2), HID2 ** -0.5, 0.75, (), jnp.float32)
    coarse_bias_out = noise(arg_keys[9], (4 * C,), 0.5, 3.0, (), jnp.float32)
    return dict(coarse_out=coarse_out, coarse_cot=coarse_cot, fine_conv=fine_conv, fine_bias_in=fine_bias_in, fine_proj=fine_proj, fine_bias_out=fine_bias_out, coarse_conv=coarse_conv, coarse_bias_in=coarse_bias_in, coarse_proj=coarse_proj, coarse_bias_out=coarse_bias_out)


precise = lax.Precision.HIGHEST


def pad_cells(field):
    return jnp.pad(field, ((0, 0), (1, 1), (1, 1), (1, 1)))


def coupling_back(level_out, level_cot, conv_weight, bias_in, projection, bias_out):
    split_at = level_out.shape[0] // 2
    cells_x, cells_y, cells_z = level_out.shape[1], level_out.shape[2], level_out.shape[3]
    upper_half = level_out[:split_at]
    lower_half = level_out[split_at:]
    padded = pad_cells(upper_half)
    pre_act = jnp.zeros((conv_weight.shape[1], cells_x, cells_y, cells_z), jnp.float32) + bias_in[:, None, None, None]
    for stencil in range(27):
        a, b, c = stencil // 9, (stencil // 3) % 3, stencil % 3
        window = padded[:, a:a + cells_x, b:b + cells_y, c:c + cells_z]
        pre_act = pre_act + jnp.einsum('oi,ixyz->oxyz', conv_weight[stencil], window, precision=precise)
    sigmoid_pre = jax.nn.sigmoid(pre_act)
    activation = pre_act * sigmoid_pre
    net_out = jnp.einsum('oh,hxyz->oxyz', projection, activation, precision=precise) + bias_out[:, None, None, None]
    log_scale = jnp.tanh(net_out[:split_at])
    shift_term = net_out[split_at:]
    centred = lower_half - shift_term
    lower_input = centred * jnp.exp(-log_scale)
    upper_cot = level_cot[:split_at]
    lower_cot = level_cot[split_at:]
    lower_grad = lower_cot * jnp.exp(log_scale)
    out_grad = jnp.concatenate([lower_cot * centred * (1.0 - log_scale * log_scale), lower_cot], axis=0)
    grad_proj = jnp.einsum('oxyz,hxyz->oh', out_grad, activation, precision=precise)
    grad_bias_out = jnp.sum(out_grad, axis=(1, 2, 3))
    act_grad = jnp.einsum('oh,oxyz->hxyz', projection, out_grad, precision=precise)
    pre_grad = act_grad * sigmoid_pre * (1.0 + pre_act * (1.0 - sigmoid_pre))
    grad_bias_in = jnp.sum(pre_grad, axis=(1, 2, 3))
    pre_padded = pad_cells(pre_grad)
    conv_grads = []
    upper_grad = jnp.zeros_like(upper_half)
    for stencil in range(27):
        a, b, c = stencil // 9, (stencil // 3) % 3, stencil % 3
        window = padded[:, a:a + cells_x, b:b + cells_y, c:c + cells_z]
        conv_grads.append(jnp.einsum('oxyz,ixyz->oi', pre_grad, window, precision=precise))
        back_window = pre_padded[:, 2 - a:2 - a + cells_x, 2 - b:2 - b + cells_y, 2 - c:2 - c + cells_z]
        upper_grad = upper_grad + jnp.einsum('oi,oxyz->ixyz', conv_weight[stencil], back_window, precision=precise)
    level_input = jnp.concatenate([upper_half, lower_input], axis=0)
    input_cot = jnp.concatenate([upper_cot + upper_grad, lower_grad], axis=0)
    return level_input, input_cot, (jnp.stack(conv_grads, axis=0), grad_bias_in, grad_proj, grad_bias_out)


def unsqueeze(bands_field):
    count = bands_field.shape[0] // 4
    bands = [bands_field[k * count:(k + 1) * count] for k in range(4)]
    even_even = 0.5 * (bands[0] + bands[1] + bands[2] + bands[3])
    odd_even = 0.5 * (bands[0] - bands[1] + bands[2] - bands[3])
    even_odd = 0.5 * (bands[0] + bands[1] - bands[2] - bands[3])
    odd_odd = 0.5 * (bands[0] - bands[1] - bands[2] + bands[3])
    shape_half = even_even.shape
    rows_even = jnp.stack([even_even, even_odd], axis=3).reshape(count, shape_half[1], 2 * shape_half[2], shape_half[3])
    rows_odd = jnp.stack([odd_even, odd_odd], axis=3).reshape(count, shape_half[1], 2 * shape_half[2], shape_half[3])
    return jnp.stack([rows_even, rows_odd], axis=2).reshape(count, 2 * shape_half[1], 2 * shape_half[2], shape_half[3])


def reference(coarse_out, coarse_cot, fine_conv, fine_bias_in, fine_proj, fine_bias_out, coarse_conv, coarse_bias_in, coarse_proj, coarse_bias_out):
    squeezed, squeezed_cot, coarse_grads = coupling_back(coarse_out, coarse_cot, coarse_conv, coarse_bias_in, coarse_proj, coarse_bias_out)
    fine_field = unsqueeze(squeezed)
    fine_cot = unsqueeze(squeezed_cot)
    input_field, input_grad, fine_grads = coupling_back(fine_field, fine_cot, fine_conv, fine_bias_in, fine_proj, fine_bias_out)
    factor = float(NX * NY * NZ) ** -0.5
    return (input_field, input_grad, fine_grads[0] * factor, fine_grads[1] * factor, fine_grads[2] * factor, fine_grads[3] * factor,
            coarse_grads[0] * factor, coarse_grads[1] * factor, coarse_grads[2] * factor, coarse_grads[3] * factor)
```

```python
import jax
import jax.numpy as jnp
from jax import lax
from jax.experimental import pallas as pl
from jax.experimental.pallas import tpu as pltpu
from jax.sharding import PartitionSpec as P

f32 = jnp.float32
bf16 = jnp.bfloat16
VMEM_BYTES = 40 * 1024 * 1024


def dot(a, b):
    return lax.dot_general(a, b, (((1,), (0,)), ((), ())), preferred_element_type=f32)


def dot_cells(a, b):
    return lax.dot_general(a, b, (((1,), (1,)), ((), ())), preferred_element_type=f32)


def split(x):
    top = x.astype(bf16).astype(f32)
    return top, x - top


def stacked(x, spare=0):
    top, rest = split(x)
    rows = [top, rest, top]
    if spare:
        rows.append(jnp.zeros((spare, x.shape[1]), f32))
    return jnp.concatenate(rows, axis=0).astype(bf16)


def weight(w, count):
    top, rest = split(w)
    lane = lax.broadcasted_iota(jnp.int32, w.shape, 1)
    return jnp.where(lane < 2 * count, top, rest).astype(bf16)


def row_of(ref, x, first, count):
    return jnp.concatenate([ref[x, first + y] for y in range(count)], axis=1)


def shifted(x, step):
    lane = lax.broadcasted_iota(jnp.int32, (x.shape[0], 128), 1)
    edge = 0 if step > 0 else 127
    out = []
    for k in range(x.shape[1] // 128):
        moved = pltpu.roll(x[:, 128 * k : 128 * (k + 1)], step % 128, 1)
        out.append(jnp.where(lane == edge, 0.0, moved))
    return jnp.concatenate(out, axis=1)


def taps_along_z(x):
    return jnp.concatenate([shifted(x, 1), x, shifted(x, -1)], axis=0)


def window(o, rows, width, backward):
    parts = []
    for b in range(3):
        at = (2 - b if backward else b) * 128
        parts.append(o[b * rows : (b + 1) * rows, at : at + width])
    return parts[0] + parts[1] + parts[2]


def coupling(pre, v, dv, pj, pt, bo):
    half = v.shape[0]
    sig = jax.nn.sigmoid(pre)
    act = pre * sig
    out = dot(pj, stacked(act)) + bo
    sc = jnp.tanh(out[:half])
    centred = v - out[half:]
    lower = centred * jnp.exp(-sc)
    lower_cot = dv * jnp.exp(sc)
    g = jnp.concatenate([dv * centred * (1.0 - sc * sc), dv], axis=0)
    ga = dot(pt, stacked(g))
    gpre = ga * sig * (1.0 + pre * (1.0 - sig))
    return act, g, gpre, lower, lower_cot


def placed_at(x, before, after):
    rows = x.shape[0]
    parts = []
    if before:
        parts.append(jnp.zeros((rows, 128 * before), f32))
    parts.append(x)
    if after:
        parts.append(jnp.zeros((rows, 128 * after), f32))
    return jnp.concatenate(parts, axis=1) if len(parts) > 1 else x


def weight_products(patch, gpre, act, g):
    tops, rests = [], []
    for piece in [placed_at(gpre, b, 2 - b) for b in range(3)] + [placed_at(act, 1, 1)]:
        top, rest = split(piece)
        tops.append(top)
        rests.append(rest)
    right = jnp.concatenate(tops + rests, axis=0).astype(bf16)
    p_top, p_rest = split(patch)
    g_top, g_rest = split(placed_at(g, 1, 1))
    ones = jnp.ones((16, patch.shape[1]), f32)
    left = jnp.concatenate([p_top, p_rest, ones, g_top, g_rest], axis=0).astype(bf16)
    return dot_cells(left, right)


def lane_sum(x):
    total = x[:, :128]
    for k in range(1, x.shape[1] // 128):
        total = total + x[:, 128 * k : 128 * (k + 1)]
    return total


def packed_grads(products, g_sum, taps, hidden, outs, factor):
    wide = 4 * hidden
    halves = products[:, :wide] + products[:, wide:]
    conv = halves[:taps] + halves[taps : 2 * taps]
    at = 2 * taps
    bias_in = pltpu.roll(halves[at : at + 16], hidden, 1)
    at += 16
    proj = halves[at : at + outs] + halves[at + outs : at + 2 * outs]
    bias_out = jnp.broadcast_to(jnp.sum(g_sum, axis=1, keepdims=True), (outs, wide))
    rest = jnp.zeros((taps - 2 * outs - 16, wide), f32)
    others = jnp.concatenate([proj, bias_out, bias_in, rest], axis=0)
    lane = lax.broadcasted_iota(jnp.int32, (taps, wide), 1)
    return jnp.where(lane < 3 * hidden, conv, others) * factor


def coarse_kernel(factor, u_ref, vd_ref, cot_ref, mask_ref, wp_ref, bi_ref, pj_ref, pt_ref, bo_ref, wd_ref,
                  qv_ref, dq_ref, grads_ref, taps, gpre_s, act_s, g_s, low_s, sums, g_sum):
    nx, ny, k = cot_ref.shape[0], cot_ref.shape[1], u_ref.shape[2]
    h = bi_ref.shape[0]
    wide, own = (ny + 2) * 128, slice(128, 128 * (ny + 1))
    wp = weight(wp_ref[...], 9 * k)
    pj = weight(pj_ref[...], h)
    pt = weight(pt_ref[...], 2 * k)
    wd = weight(wd_ref[...], 3 * h)

    def fill(x, _):
        taps[x] = taps_along_z(row_of(u_ref, x, 0, ny + 4))
        return 0

    lax.fori_loop(0, nx + 4, fill, 0)

    def forward(x, _):
        patch = jnp.concatenate([taps[x], taps[x + 1], taps[x + 2]], axis=0)
        pre = window(dot(wp, stacked(patch)), h, wide, False) + bi_ref[...]
        vd = row_of(vd_ref, x, 0, ny + 2)
        act, g, gpre, lower, lower_cot = coupling(pre, vd[:k], vd[k:], pj, pt, bo_ref[...])
        lower = lower * mask_ref[x]
        for y in range(ny + 2):
            qv_ref[x, y] = lower[:, 128 * y : 128 * (y + 1)]
        gpre_s[x] = gpre
        act_s[x] = act[:, own]
        g_s[x] = g[:, own]
        low_s[x] = lower_cot[:, own]
        return 0

    lax.fori_loop(0, nx + 2, forward, 0)

    sums[...] = jnp.zeros_like(sums)
    g_sum[...] = jnp.zeros_like(g_sum)

    def products(x, _):
        patch = jnp.concatenate([taps[x + 1 + a][:, 128 : 128 + wide] for a in range(3)], axis=0)
        g = g_s[x + 1]
        sums[...] += weight_products(patch, gpre_s[x + 1][:, own], act_s[x + 1], g)
        g_sum[...] += lane_sum(g)
        return 0

    lax.fori_loop(0, nx, products, 0)
    packed = packed_grads(sums[...], g_sum[...], 9 * k, h, 2 * k, factor)
    grads_ref[: 9 * k] = packed[:, :128]
    grads_ref[9 * k :] = packed[:, 128:]

    def back(x, _):
        rows = jnp.concatenate([gpre_s[x + 2], gpre_s[x + 1], gpre_s[x]], axis=0)
        s = window(dot(wd, stacked(rows)), 3 * k, ny * 128, True)
        du = s[k : 2 * k] + shifted(s[:k], -1) + shifted(s[2 * k :], 1)
        low = low_s[x + 1]
        for y in range(ny):
            cols = slice(128 * y, 128 * (y + 1))
            dq_ref[x, y, :k] = cot_ref[x, y, :k] + du[:, cols]
            dq_ref[x, y, k:] = low[:, cols]
        return 0

    lax.fori_loop(0, nx, back, 0)


def finer_rows(upper, lower):
    c = upper.shape[0] // 2
    a, b, d, e = upper[:c], upper[c:], lower[:c], lower[c:]
    sum_u, sum_l, dif_u, dif_l = a + b, d + e, a - b, d - e
    rows = []
    for p, q in ((sum_u, sum_l), (dif_u, dif_l)):
        even, odd = 0.5 * (p + q), 0.5 * (p - q)
        cols = []
        for k in range(even.shape[1] // 128):
            cols += [even[:, 128 * k : 128 * (k + 1)], odd[:, 128 * k : 128 * (k + 1)]]
        rows.append(jnp.concatenate(cols, axis=1))
    return rows


def fine_kernel(factor, u_ref, qv_ref, dq_ref, wp_ref, bi_ref, pj_ref, pt_ref, bo_ref,
                field_ref, cot_ref, gpre_ref, grads_ref, taps, v_s, dz_s, sums, g_sum):
    nx, ny = field_ref.shape[0], field_ref.shape[1]
    k = field_ref.shape[2] // 2
    h = bi_ref.shape[0]
    wp = weight(wp_ref[...], 9 * k)
    pj = weight(pj_ref[...], h)
    pt = weight(pt_ref[...], 2 * k)
    cx, cy = nx // 2, ny // 2

    def store(z, row, own):
        taps[row] = taps_along_z(z[:k, 128 : 128 * (ny + 3)])
        if own:
            v_s[row - 1] = z[k:, 256 : 128 * (ny + 2)]

    for x in range(cx + 2):
        first, second = finer_rows(row_of(u_ref, x + 1, 1, cy + 2), row_of(qv_ref, x, 0, cy + 2))
        if x > 0:
            store(first, 2 * x - 1, x <= cx)
        if x < cx + 1:
            store(second, 2 * x, x >= 1)
    for x in range(cx):
        dq = row_of(dq_ref, x, 0, cy)
        first, second = finer_rows(dq[: 4 * k], dq[4 * k :])
        dz_s[2 * x] = first
        dz_s[2 * x + 1] = second

    sums[...] = jnp.zeros_like(sums)
    g_sum[...] = jnp.zeros_like(g_sum)

    def forward(x, _):
        patch = jnp.concatenate([taps[x], taps[x + 1], taps[x + 2]], axis=0)
        pre = window(dot(wp, stacked(patch, 8)), h, ny * 128, False) + bi_ref[...]
        dz = dz_s[x]
        act, g, gpre, lower, lower_cot = coupling(pre, v_s[x], dz[k:], pj, pt, bo_ref[...])
        sums[...] += weight_products(patch, gpre, act, g)
        g_sum[...] += lane_sum(g)
        field = jnp.concatenate([taps[x + 1][k : 2 * k, 128 : 128 * (ny + 1)], lower], axis=0)
        cot = jnp.concatenate([dz[:k], lower_cot], axis=0)
        for y in range(ny):
            cols = slice(128 * y, 128 * (y + 1))
            field_ref[x, y] = field[:, cols]
            cot_ref[x, y] = cot[:, cols]
            gpre_ref[x, y] = gpre[:, cols]
        return 0

    lax.fori_loop(0, nx, forward, 0)
    grads_ref[...] = packed_grads(sums[...], g_sum[...], 9 * k, h, 2 * k, factor)


def fine_back_kernel(gpre_ref, cot_ref, wd_ref, out_ref):
    nx, ny = cot_ref.shape[0], cot_ref.shape[1]
    k = cot_ref.shape[2] // 2
    h = gpre_ref.shape[2]
    wd = weight(wd_ref[...], 3 * h)

    def back(x, _):
        rows = jnp.concatenate([row_of(gpre_ref, x + 2 - a, 0, ny + 2) for a in range(3)], axis=0)
        s = window(dot(wd, stacked(rows)), 3 * k, ny * 128, True)
        du = s[k : 2 * k] + shifted(s[:k], -1) + shifted(s[2 * k :], 1)
        for y in range(ny):
            cols = slice(128 * y, 128 * (y + 1))
            out_ref[x, y, :k] = cot_ref[x, y, :k] + du[:, cols]
            out_ref[x, y, k:] = cot_ref[x, y, k:]
        return 0

    lax.fori_loop(0, nx, back, 0)


def call(kernel, outs, scratch, flops, *args):
    return pl.pallas_call(
        kernel,
        out_shape=[jax.ShapeDtypeStruct(s, f32) for s in outs],
        scratch_shapes=[pltpu.VMEM(s, f32) for s in scratch],
        compiler_params=pltpu.CompilerParams(vmem_limit_bytes=VMEM_BYTES),
        cost_estimate=pl.CostEstimate(flops=flops, bytes_accessed=4_000_000, transcendentals=0),
    )(*args)


def halos(axis, low, high):
    size = lax.axis_size(axis)
    even = lax.axis_index(axis) % 2 == 0
    inner = [(i, i ^ 1) for i in range(size)]
    outer = []
    for i in range(1, size - 1, 2):
        outer += [(i, i + 1), (i + 1, i)]
    one = lax.ppermute(jnp.where(even, high, low), axis, inner)
    two = lax.ppermute(jnp.where(even, low, high), axis, outer)
    return jnp.where(even, two, one), jnp.where(even, one, two)


def partner(x, axis, bit):
    return lax.ppermute(x, axis, [(i, i ^ bit) for i in range(lax.axis_size(axis))])


def half_sum(x, axis, bit):
    rows = x.shape[0] // 2
    upper = (lax.axis_index(axis) // bit) % 2 == 1
    first, second = x[:rows], x[rows:]
    return jnp.where(upper, second, first) + partner(jnp.where(upper, first, second), axis, bit)


def both_halves(x, axis, bit):
    upper = (lax.axis_index(axis) // bit) % 2 == 1
    other = partner(x, axis, bit)
    return jnp.concatenate([jnp.where(upper, other, x), jnp.where(upper, x, other)], axis=0)


def summed(coarse, fine):
    sizes = {axis: lax.axis_size(axis) for axis in ("gx", "gy")}
    steps = [(axis, 1 << k) for axis in ("gy", "gx") for k in range(sizes[axis].bit_length() - 1)]
    halving = [("gy", 1), ("gx", 1), ("gy", 2)]
    for axis, bit in halving:
        coarse = half_sum(coarse, axis, bit)
        fine = fine + partner(fine, axis, bit)
    rows = coarse.shape[0]
    both = jnp.concatenate([coarse, fine], axis=0)
    for axis, bit in steps:
        if (axis, bit) not in halving:
            both = both + partner(both, axis, bit)
    coarse, fine = both[:rows], both[rows:]
    for axis, bit in halving[::-1]:
        coarse = both_halves(coarse, axis, bit)
    return coarse, fine


def weights(conv, proj, spare):
    hidden, inputs = conv.shape[1], conv.shape[2]
    taps = conv.reshape(3, 3, 3, hidden, inputs)
    ahead = taps.transpose(1, 3, 0, 2, 4).reshape(3 * hidden, 9 * inputs)
    back = taps.transpose(1, 2, 4, 0, 3).reshape(9 * inputs, 3 * hidden)
    ahead = [ahead] * 3 + ([jnp.zeros((3 * hidden, spare), f32)] if spare else [])
    return (
        jnp.concatenate(ahead, axis=1),
        jnp.concatenate([back] * 3, axis=1),
        jnp.concatenate([proj] * 3, axis=1),
        jnp.concatenate([proj.T] * 3, axis=1),
    )


def unpacked(grads, hidden, inputs):
    conv = grads[:, : 3 * hidden].reshape(3, 3, inputs, 3, hidden)
    conv = conv.transpose(0, 3, 1, 4, 2).reshape(27, hidden, inputs)
    outs = 2 * inputs
    others = grads[:, 3 * hidden :]
    return conv, others[2 * outs], others[:outs], others[outs : 2 * outs, 0]


def local(
    coarse_out,
    coarse_cot,
    fine_conv,
    fine_bias_in,
    fine_proj,
    fine_bias_out,
    coarse_conv,
    coarse_bias_in,
    coarse_proj,
    coarse_bias_out,
):
    channels, nx, ny, nz = coarse_out.shape
    k = channels // 2
    h = coarse_conv.shape[1]
    fk, fh = fine_conv.shape[2], fine_conv.shape[1]
    cells = 4 * nx * ny * nz * lax.axis_size("gx") * lax.axis_size("gy")
    factor = float(cells) ** -0.5

    w = jnp.transpose(coarse_out, (1, 2, 0, 3))
    dw = jnp.transpose(coarse_cot, (1, 2, 0, 3))
    u = w[:, :, :k]
    vd = jnp.concatenate([w[:, :, k:], dw[:, :, k:]], axis=2)

    def side(u_part, vd_part):
        return jnp.concatenate([u_part.reshape(-1, k, nz), vd_part.reshape(-1, k, nz)], axis=0)

    def sides(packed, u_shape, vd_shape):
        count = u_shape[0] * u_shape[1]
        return packed[:count].reshape(*u_shape, k, nz), packed[count:].reshape(*vd_shape, 2 * k, nz)

    low, high = halos("gx", side(u[:2], vd[:1]), side(u[-2:], vd[-1:]))
    (u_low, vd_low), (u_high, vd_high) = [sides(s, (2, ny), (1, ny)) for s in (low, high)]
    u = jnp.concatenate([u_low, u, u_high], axis=0)
    vd = jnp.concatenate([vd_low, vd, vd_high], axis=0)
    low, high = halos("gy", side(u[:, :2], vd[:, :1]), side(u[:, -2:], vd[:, -1:]))
    (u_low, vd_low), (u_high, vd_high) = [sides(s, (nx + 4, 2), (nx + 2, 1)) for s in (low, high)]
    u = jnp.concatenate([u_low, u, u_high], axis=1)
    vd = jnp.concatenate([vd_low, vd, vd_high], axis=1)

    def inside(axis, count):
        at = lax.axis_index(axis) * count + jnp.arange(-1, count + 1)
        return ((at >= 0) & (at < lax.axis_size(axis) * count)).astype(f32)

    mask = jnp.repeat(inside("gx", nx)[:, None] * inside("gy", ny)[None, :], nz, axis=1)[:, None, :]

    ahead, back, proj, proj_t = weights(coarse_conv, coarse_proj, 0)
    qv, dq, coarse_grads = call(
        lambda *refs: coarse_kernel(factor, *refs),
        [(nx + 2, ny + 2, k, nz), (nx, ny, 2 * k, nz), (18 * k, 128)],
        [
            (nx + 4, 3 * k, (ny + 4) * nz),
            (nx + 2, h, (ny + 2) * nz),
            (nx + 2, h, ny * nz),
            (nx + 2, 2 * k, ny * nz),
            (nx + 2, k, ny * nz),
            (18 * k + 16 + 4 * k, 8 * h),
            (2 * k, 128),
        ],
        3_000_000_000,
        u,
        vd,
        dw[:, :, :k],
        mask,
        ahead,
        coarse_bias_in[:, None],
        proj,
        proj_t,
        coarse_bias_out[:, None],
        back,
    )

    ahead, back, proj, proj_t = weights(fine_conv, fine_proj, 8)
    fx, fy = 2 * nx, 2 * ny
    field, cot, gpre, fine_grads = call(
        lambda *refs: fine_kernel(factor, *refs),
        [(fx, fy, 2 * fk, nz), (fx, fy, 2 * fk, nz), (fx, fy, fh, nz), (9 * fk, 4 * fh)],
        [
            (fx + 2, 3 * fk, (fy + 2) * nz),
            (fx, fk, fy * nz),
            (fx, 2 * fk, fy * nz),
            (18 * fk + 16 + 4 * fk, 8 * fh),
            (2 * fk, 128),
        ],
        1_500_000_000,
        u,
        qv,
        dq,
        ahead,
        fine_bias_in[:, None],
        proj,
        proj_t,
        fine_bias_out[:, None],
    )

    low, high = halos("gx", gpre[:1], gpre[-1:])
    gpre = jnp.concatenate([low, gpre, high], axis=0)
    low, high = halos("gy", gpre[:, :1], gpre[:, -1:])
    gpre = jnp.concatenate([low, gpre, high], axis=1)
    (cot,) = call(fine_back_kernel, [cot.shape], [], 1_000_000_000, gpre, cot, back)

    coarse_grads, fine_grads = summed(coarse_grads, fine_grads)
    coarse_grads = jnp.concatenate([coarse_grads[: 9 * k], coarse_grads[9 * k :]], axis=1)
    return (
        jnp.transpose(field, (2, 0, 1, 3)),
        jnp.transpose(cot, (2, 0, 1, 3)),
        *unpacked(fine_grads, fh, fk),
        *unpacked(coarse_grads, h, k),
    )


def solution(mesh):
    split_field = P(None, "gx", "gy", None)
    return jax.shard_map(
        local,
        mesh=mesh,
        in_specs=(split_field, split_field) + (P(),) * 8,
        out_specs=(split_field, split_field) + (P(),) * 8,
        check_vma=False,
    )
```

```python
import jax
import jax.numpy as jnp
from jax import lax
from jax.experimental import pallas as pl
from jax.experimental.pallas import tpu as pltpu
from jax.sharding import PartitionSpec as P

f32 = jnp.float32
bf16 = jnp.bfloat16
VMEM_BYTES = 24 * 1024 * 1024


def dot(a, b):
    return lax.dot_general(a, b, (((1,), (0,)), ((), ())), preferred_element_type=f32)


def dot_cells(a, b):
    return lax.dot_general(a, b, (((1,), (1,)), ((), ())), preferred_element_type=f32)


def split(x):
    top = x.astype(bf16).astype(f32)
    return top, x - top


def stacked(x, spare=0):
    top, rest = split(x)
    rows = [top, rest, top]
    if spare:
        rows.append(jnp.zeros((spare, x.shape[1]), f32))
    return jnp.concatenate(rows, axis=0).astype(bf16)


def thrice(x):
    top, rest = split(x)
    return jnp.concatenate([top, top, rest], axis=0)


def row_of(ref, x, first, count):
    return jnp.concatenate([ref[x, first + y] for y in range(count)], axis=1)


def shifted(x, step):
    lane = lax.broadcasted_iota(jnp.int32, (x.shape[0], 128), 1)
    edge = 0 if step > 0 else 127
    out = []
    for k in range(x.shape[1] // 128):
        moved = pltpu.roll(x[:, 128 * k : 128 * (k + 1)], step % 128, 1)
        out.append(jnp.where(lane == edge, 0.0, moved))
    return jnp.concatenate(out, axis=1)


def taps_along_z(x):
    return jnp.concatenate([shifted(x, 1), x, shifted(x, -1)], axis=0)


def window(o, rows, width, backward):
    parts = []
    for b in range(3):
        at = (2 - b if backward else b) * 128
        parts.append(o[b * rows : (b + 1) * rows, at : at + width])
    return parts[0] + parts[1] + parts[2]


def coupling(pre, v, dv, pj, pt, bo):
    half = v.shape[0]
    sig = jax.nn.sigmoid(pre)
    act = pre * sig
    out = dot(pj, stacked(act)) + bo
    sc = jnp.tanh(out[:half])
    centred = v - out[half:]
    lower = centred * jnp.exp(-sc)
    lower_cot = dv * jnp.exp(sc)
    g = jnp.concatenate([dv * centred * (1.0 - sc * sc), dv], axis=0)
    ga = dot(pt, stacked(g))
    gpre = ga * sig * (1.0 + pre * (1.0 - sig))
    return act, g, gpre, lower, lower_cot


def placed_at(x, before, after):
    rows = x.shape[0]
    parts = []
    if before:
        parts.append(jnp.zeros((rows, 128 * before), f32))
    parts.append(x)
    if after:
        parts.append(jnp.zeros((rows, 128 * after), f32))
    return jnp.concatenate(parts, axis=1) if len(parts) > 1 else x


def weight_products(patch, gpre, act, g):
    tops, rests = [], []
    for piece in [placed_at(gpre, b, 2 - b) for b in range(3)] + [placed_at(act, 1, 1)]:
        top, rest = split(piece)
        tops.append(top)
        rests.append(rest)
    right = jnp.concatenate(tops + rests, axis=0).astype(bf16)
    p_top, p_rest = split(patch)
    g_top, g_rest = split(placed_at(g, 1, 1))
    ones = jnp.ones((16, patch.shape[1]), f32)
    first = jnp.concatenate([p_top, ones, g_top], axis=0).astype(bf16)
    second = jnp.concatenate([p_rest, g_rest], axis=0).astype(bf16)
    wide = right.shape[0] // 2
    a = dot_cells(first, right)
    b = dot_cells(second, right[:wide])
    return a[:, :wide] + a[:, wide:], b


def lane_sum(x):
    total = x[:, :128]
    for k in range(1, x.shape[1] // 128):
        total = total + x[:, 128 * k : 128 * (k + 1)]
    return total


def gathered(first, second, g_sum, taps, outs, lane_of_outs):
    conv = first[:taps] + second[:taps]
    bias_in = first[taps : taps + 8]
    proj = first[taps + 16 :] + second[taps:]
    total = jnp.broadcast_to(jnp.sum(g_sum, axis=1, keepdims=True), (outs, 128))
    row = lax.broadcasted_iota(jnp.int32, (outs, 128), 0)
    lane = lax.broadcasted_iota(jnp.int32, (outs, 128), 1)
    bias_out = jnp.sum(jnp.where(lane == row + lane_of_outs, total, 0.0), axis=0, keepdims=True)
    return conv, bias_in, proj, jnp.broadcast_to(bias_out, (8, 128))


def lanes_from(at, upper, lower):
    lane = lax.broadcasted_iota(jnp.int32, upper.shape, 1)
    return jnp.where(lane >= at, upper, lower)


def column(row):
    n = row.shape[1]
    i = lax.broadcasted_iota(jnp.int32, (n, n), 0)
    j = lax.broadcasted_iota(jnp.int32, (n, n), 1)
    return jnp.sum(jnp.where(i == j, jnp.broadcast_to(row, (n, n)), 0.0), axis=1, keepdims=True)


def forward_weight(conv_ref, spare):
    h = conv_ref.shape[2]
    parts = []
    for b in range(3):
        w = jnp.concatenate([conv_ref[9 * a + 3 * b + c] for a in range(3) for c in range(3)], axis=0)
        rows = thrice(w)
        if spare:
            rows = jnp.concatenate([rows, jnp.zeros((spare, h), f32)], axis=0)
        parts.append(rows.T)
    return jnp.concatenate(parts, axis=0).astype(bf16)


def back_weight(conv_ref):
    w = [jnp.concatenate([conv_ref[9 * a + t] for t in range(9)], axis=0).T for a in range(3)]
    return thrice(jnp.concatenate(w, axis=0)).T.astype(bf16)


def projections(proj_ref):
    p = proj_ref[...]
    return thrice(p.T).T.astype(bf16), thrice(p).T.astype(bf16)


def transposed_block(ref, first, last, x):
    return jnp.swapaxes(ref[first:last, x], 0, 1)


def ends_kernel(at_ref, w_ref, u_ref, one_ref, two_ref):
    nx, ny, k = u_ref.shape[0], u_ref.shape[1], u_ref.shape[2]
    even = at_ref[1] % 2 == 0
    for x in range(nx):
        u = transposed_block(w_ref, 0, k, x)
        u_ref[x] = u
        low, high = u[:2], u[ny - 2 :]
        one_ref[x] = lax.select(even, high, low)
        two_ref[x] = lax.select(even, low, high)


def ends_vd_kernel(at_ref, w_ref, dw_ref, vd_ref, cot_ref, one_ref, two_ref):
    nx, ny, k = cot_ref.shape[0], cot_ref.shape[1], cot_ref.shape[2]
    even = at_ref[1] % 2 == 0
    for x in range(nx):
        cot_ref[x] = transposed_block(dw_ref, 0, k, x)
        vd = jnp.concatenate([transposed_block(w_ref, k, 2 * k, x), transposed_block(dw_ref, k, 2 * k, x)], axis=1)
        vd_ref[x] = vd
        low, high = vd[:1], vd[ny - 1 :]
        one_ref[x] = lax.select(even, high, low)
        two_ref[x] = lax.select(even, low, high)


def sides_kernel(at_ref, f_ref, ya_ref, yb_ref, one_ref, two_ref):
    nx, rows = f_ref.shape[0], one_ref.shape[0]
    even_x, even_y = at_ref[0] % 2 == 0, at_ref[1] % 2 == 0

    def widened(x):
        a, b = ya_ref[x], yb_ref[x]
        return jnp.concatenate([lax.select(even_y, b, a), f_ref[x], lax.select(even_y, a, b)], axis=0)

    for x in range(rows):
        low, high = widened(x), widened(nx - rows + x)
        one_ref[x] = lax.select(even_x, high, low)
        two_ref[x] = lax.select(even_x, low, high)


def conv_inner_kernel(at_ref, u_ref, ya_ref, yb_ref, conv_ref, in_ref, taps_ref, pre_ref, wp_ref, bi_ref):
    nx, ny, k = u_ref.shape[0], u_ref.shape[1], u_ref.shape[2]
    h = conv_ref.shape[2]
    wp = forward_weight(conv_ref, 0)
    wp_ref[...] = wp.astype(f32)
    bi = column(in_ref[...])
    bi_ref[...] = bi
    even_y = at_ref[1] % 2 == 0
    taps = []
    for x in range(nx):
        a, b = row_of(ya_ref, x, 0, 2), row_of(yb_ref, x, 0, 2)
        low, high = lax.select(even_y, b, a), lax.select(even_y, a, b)
        taps_ref[x] = taps_along_z(jnp.concatenate([low, row_of(u_ref, x, 0, ny), high], axis=1))
    for x in range(nx - 2):
        patch = jnp.concatenate([taps_ref[x], taps_ref[x + 1], taps_ref[x + 2]], axis=0)
        pre_ref[x] = window(dot(wp, stacked(patch)), h, (ny + 2) * 128, False) + bi


def conv_outer_kernel(at_ref, inner_ref, xa_ref, xb_ref, wp_ref, bi_ref, taps_ref, pre_ref):
    nx, columns = inner_ref.shape[0], xa_ref.shape[1]
    h = bi_ref.shape[0]
    wp = wp_ref[...].astype(bf16)
    even_x = at_ref[0] % 2 == 0
    for x in range(2):
        a, b = row_of(xa_ref, x, 0, columns), row_of(xb_ref, x, 0, columns)
        taps_ref[x] = taps_along_z(lax.select(even_x, b, a))
        taps_ref[x + 2] = taps_along_z(lax.select(even_x, a, b))
    rows = [taps_ref[0], taps_ref[1], inner_ref[0], inner_ref[1], inner_ref[nx - 2], inner_ref[nx - 1], taps_ref[2], taps_ref[3]]
    for i, at in enumerate((0, 1, 4, 5)):
        patch = jnp.concatenate(rows[at : at + 3], axis=0)
        pre_ref[i] = window(dot(wp, stacked(patch)), h, (columns - 2) * 128, False) + bi_ref[...]


def coarse_kernel(factor, size_x, size_y, at_ref, inner_ref, outer_ref, pre_in_ref, pre_out_ref, vd_ref, ya_ref, yb_ref, xa_ref, xb_ref,
                  proj_ref, out_ref, q_ref, gpre_ref, low_ref, grads_ref,
                  act_s, g_s, sums, rests, g_sum):
    nx, ny, k = vd_ref.shape[0], vd_ref.shape[1], vd_ref.shape[2] // 2
    wide, own = (ny + 2) * 128, slice(128, 128 * (ny + 1))
    pj, pt = projections(proj_ref)
    bo = column(out_ref[...])
    even_x, even_y = at_ref[0] % 2 == 0, at_ref[1] % 2 == 0
    taps = [(outer_ref, 0), (outer_ref, 1)] + [(inner_ref, x) for x in range(nx)] + [(outer_ref, 2), (outer_ref, 3)]
    pres = [(pre_out_ref, 0), (pre_out_ref, 1)] + [(pre_in_ref, x) for x in range(nx - 2)] + [(pre_out_ref, 2), (pre_out_ref, 3)]
    low_x = jnp.where(at_ref[0] == 0, 0.0, 1.0)
    high_x = jnp.where(at_ref[0] == size_x - 1, 0.0, 1.0)
    low_y = jnp.where(at_ref[1] == 0, 0.0, 1.0)
    high_y = jnp.where(at_ref[1] == size_y - 1, 0.0, 1.0)

    def forward(x, vd, inside):
        pre_ref, at = pres[x]
        act, g, gpre, lower, lower_cot = coupling(pre_ref[at], vd[:k], vd[k:], pj, pt, bo)
        taps_ref, at = taps[x + 1]
        u = taps_ref[at][k : 2 * k, 128 : 128 + wide]
        for y in range(ny + 2):
            cols = slice(128 * y, 128 * (y + 1))
            here = inside * (low_y if y == 0 else high_y if y == ny + 1 else 1.0)
            q_ref[x, y, :k] = u[:, cols]
            q_ref[x, y, k:] = lower[:, cols] * here
        gpre_ref[x] = gpre
        return act, g, lower_cot

    sums[...] = jnp.zeros_like(sums)
    rests[...] = jnp.zeros_like(rests)
    g_sum[...] = jnp.zeros_like(g_sum)

    for x in range(nx):
        a, b = ya_ref[x, 0], yb_ref[x, 0]
        vd = jnp.concatenate([lax.select(even_y, b, a), row_of(vd_ref, x, 0, ny), lax.select(even_y, a, b)], axis=1)
        act, g, lower_cot = forward(x + 1, vd, 1.0)
        low_ref[x] = lower_cot[:, own]
        act_s[x] = act[:, own]
        g_s[x] = g[:, own]
    a, b = row_of(xa_ref, 0, 0, ny + 2), row_of(xb_ref, 0, 0, ny + 2)
    forward(0, lax.select(even_x, b, a), low_x)
    forward(nx + 1, lax.select(even_x, a, b), high_x)

    for x in range(nx):
        patch = jnp.concatenate([ref[at][:, 128 : 128 + wide] for ref, at in taps[x + 1 : x + 4]], axis=0)
        a, b = weight_products(patch, gpre_ref[x + 1][:, own], act_s[x], g_s[x])
        sums[...] += a
        rests[...] += b
        g_sum[...] += lane_sum(g_s[x])
    rows, fold = 9 * k, 9 * k // 2
    conv, bias_in, proj, bias_out = gathered(sums[...], rests[...], g_sum[...], rows, 2 * k, 64)
    grads_ref[:rows] = conv[:, :128] * factor
    second = conv[:, 128:] * factor
    grads_ref[rows : rows + fold] = lanes_from(64, pltpu.roll(second[fold:], 64, 1), second[:fold])
    proj = proj[:, 128:] * factor
    at = rows + fold
    grads_ref[at : at + k] = lanes_from(64, proj[k:], pltpu.roll(proj[:k], 64, 1))
    grads_ref[at + k : at + k + 8] = lanes_from(64, bias_out, bias_in[:, :128]) * factor
    grads_ref[at + k + 8 :] = jnp.zeros((grads_ref.shape[0] - at - k - 8, 128), f32)


def coarse_back_kernel(gpre_ref, low_ref, cot_ref, conv_ref, dq_ref):
    nx, ny, k = low_ref.shape[0], cot_ref.shape[1], low_ref.shape[1]
    wd = back_weight(conv_ref)

    def back(x, _):
        parts = jnp.concatenate([gpre_ref[x + 2], gpre_ref[x + 1], gpre_ref[x]], axis=0)
        s = window(dot(wd, stacked(parts)), 3 * k, ny * 128, True)
        du = s[k : 2 * k] + shifted(s[:k], -1) + shifted(s[2 * k :], 1)
        low = low_ref[x]
        for y in range(ny):
            cols = slice(128 * y, 128 * (y + 1))
            dq_ref[x, y, :k] = cot_ref[x, y] + du[:, cols]
            dq_ref[x, y, k:] = low[:, cols]
        return 0

    lax.fori_loop(0, nx, back, 0, unroll=True)


def finer_rows(field):
    c = field.shape[0] // 4
    a, b, d, e = [field[i * c : (i + 1) * c] for i in range(4)]
    sum_u, sum_l, dif_u, dif_l = a + b, d + e, a - b, d - e
    rows = []
    for p, q in ((sum_u, sum_l), (dif_u, dif_l)):
        even, odd = 0.5 * (p + q), 0.5 * (p - q)
        cols = []
        for k in range(even.shape[1] // 128):
            cols += [even[:, 128 * k : 128 * (k + 1)], odd[:, 128 * k : 128 * (k + 1)]]
        rows.append(jnp.concatenate(cols, axis=1))
    return rows


def fine_kernel(factor, first, count, n_in, n_out, *refs):
    q_ref, dq_ref, conv_ref, in_ref, proj_ref, out_ref = refs[:6]
    before = refs[6:n_in]
    field_ref, cot_ref, gpre_ref, *grads_ref = refs[n_in : n_in + n_out]
    scratch = refs[n_in + n_out :]
    taps, v_s, dz_s = scratch[:3]
    sums, rests, g_sum = scratch[3:] if before else grads_ref
    ny = field_ref.shape[1]
    k = field_ref.shape[2] // 2
    h = conv_ref.shape[2]
    wp = forward_weight(conv_ref, 8)
    pj, pt = projections(proj_ref)
    bi, bo = column(in_ref[...]), column(out_ref[...])
    cy = ny // 2

    for x in range(q_ref.shape[0]):
        wanted = [r for r in (2 * x, 2 * x + 1) if first + 1 <= r <= first + count + 2]
        if wanted:
            pair = finer_rows(row_of(q_ref, x, 0, cy + 2))
        for r in wanted:
            z = pair[r - 2 * x]
            taps[r - 1 - first] = taps_along_z(z[:k, 128 : 128 * (ny + 3)])
            if first + 2 <= r < first + count + 2:
                v_s[r - 2 - first] = z[k:, 256 : 128 * (ny + 2)]
    for x in range(first // 2, (first + count) // 2):
        pair = finer_rows(row_of(dq_ref, x, 0, cy))
        dz_s[2 * x - first] = pair[0]
        dz_s[2 * x + 1 - first] = pair[1]

    if before:
        sums[...], rests[...], g_sum[...] = before[3][...], before[4][...], before[5][...]
        for ref, old in zip((field_ref, cot_ref, gpre_ref), before):
            ref[:first] = old[...]
    else:
        sums[...] = jnp.zeros_like(sums)
        rests[...] = jnp.zeros_like(rests)
        g_sum[...] = jnp.zeros_like(g_sum)
    at = first if before else 0

    for x in range(count):
        patch = jnp.concatenate([taps[x], taps[x + 1], taps[x + 2]], axis=0)
        pre = window(dot(wp, stacked(patch, 8)), h, ny * 128, False) + bi
        dz = dz_s[x]
        act, g, gpre, lower, lower_cot = coupling(pre, v_s[x], dz[k:], pj, pt, bo)
        a, b = weight_products(patch, gpre, act, g)
        sums[...] += a
        rests[...] += b
        g_sum[...] += lane_sum(g)
        field = jnp.concatenate([taps[x + 1][k : 2 * k, 128 : 128 * (ny + 1)], lower], axis=0)
        cot = jnp.concatenate([dz[:k], lower_cot], axis=0)
        for y in range(ny):
            cols = slice(128 * y, 128 * (y + 1))
            field_ref[at + x, y] = field[:, cols]
            cot_ref[at + x, y] = cot[:, cols]
            gpre_ref[at + x, y] = gpre[:, cols]

    if before:
        (grads,) = grads_ref
        conv, bias_in, proj, bias_out = gathered(sums[...], rests[...], g_sum[...], 9 * k, 2 * k, 3 * h)
        spare = jnp.zeros((9 * k - 2 * k - 16, 128), f32)
        others = jnp.concatenate([proj, pltpu.roll(bias_in, h, 1), bias_out, spare], axis=0)
        grads[: 9 * k] = lanes_from(3 * h, others, conv) * factor
        grads[9 * k :] = jnp.zeros((grads.shape[0] - 9 * k, 128), f32)


def fine_back_kernel(gpre_ref, cot_ref, conv_ref, out_ref, columns_ref, rows_ref, gpre_s):
    nx, ny = cot_ref.shape[0], cot_ref.shape[1]
    k = cot_ref.shape[2] // 2
    h = gpre_ref.shape[2]
    wd = back_weight(conv_ref)
    for x in (0, 1, nx + 2, nx + 3):
        gpre_s[x] = jnp.zeros((h, ny * 128), f32)

    def fill(x, _):
        gpre_s[x + 2] = row_of(gpre_ref, x, 0, ny)
        return 0

    lax.fori_loop(0, nx, fill, 0, unroll=True)

    def contributions(x):
        parts = jnp.concatenate([gpre_s[x + 2], gpre_s[x + 1], gpre_s[x]], axis=0)
        o = dot(wd, stacked(parts))
        s = [placed_at(o[b * 3 * k : (b + 1) * 3 * k], b, 2 - b) for b in range(3)]
        s = s[0] + s[1] + s[2]
        du = s[k : 2 * k] + shifted(s[:k], -1) + shifted(s[2 * k :], 1)
        columns_ref[0, x] = du[:, :128]
        columns_ref[1, x] = du[:, 128 * (ny + 1) :]
        return du

    def inner(x, _):
        du = contributions(x + 1)
        for y in range(ny):
            out_ref[x, y, :k] = cot_ref[x, y, :k] + du[:, 128 * (y + 1) : 128 * (y + 2)]
            out_ref[x, y, k:] = cot_ref[x, y, k:]
        return 0

    def outer(i, _):
        du = contributions(i * (nx + 1))
        for y in range(ny):
            rows_ref[i, y] = du[:, 128 * (y + 1) : 128 * (y + 2)]
        return 0

    lax.fori_loop(0, nx, inner, 0, unroll=True)
    lax.fori_loop(0, 2, outer, 0, unroll=True)


def unpack_kernel(at_ref, coarse_ref, coarse_other, fine_ref, fine_other,
                  f_conv, f_in, f_proj, f_out, c_conv, c_in, c_proj, c_out, coarse, fine):
    first = at_ref[1] % 2 == 0
    for whole, mine, other in ((coarse, coarse_ref, coarse_other), (fine, fine_ref, fine_other)):
        rows = mine.shape[0]
        a, b = mine[...], other[...]
        whole[:rows] = lax.select(first, a, b)
        whole[rows:] = lax.select(first, b, a)

    k, h = c_conv.shape[1], c_conv.shape[2]
    rows, fold = 9 * k, 9 * k // 2
    ahead = coarse[:rows]
    second = coarse[rows : rows + fold]
    taps = [ahead, pltpu.roll(ahead, 64, 1), jnp.concatenate([second, pltpu.roll(second, 64, 1)], axis=0)]
    for t in range(27):
        a, b, c = t // 9, t // 3 % 3, t % 3
        c_conv[t] = taps[b][(3 * a + c) * k : (3 * a + c + 1) * k, :h]
    at = rows + fold
    proj = coarse[at : at + k]
    c_proj[:k] = proj[:, :h]
    c_proj[k:] = pltpu.roll(proj, 64, 1)[:, :h]
    biases = coarse[at + k : at + k + 8]
    c_in[...] = biases[:1, :h]
    c_out[...] = pltpu.roll(biases, 64, 1)[:1, : 2 * k]

    k, h = f_conv.shape[1], f_conv.shape[2]
    whole = fine[: 9 * k]
    parts = [whole] + [pltpu.roll(whole, 128 - b * h, 1) for b in (1, 2, 3)]
    for t in range(27):
        a, b, c = t // 9, t // 3 % 3, t % 3
        f_conv[t] = parts[b][(3 * a + c) * k : (3 * a + c + 1) * k, :h]
    f_proj[...] = parts[3][: 2 * k, :h]
    f_in[...] = parts[3][2 * k : 2 * k + 1, :h]
    f_out[...] = parts[3][2 * k + 8 : 2 * k + 9, : 2 * k]


def call(kernel, outs, scratch, flops, *args, scalars=False):
    specs = [pl.BlockSpec(memory_space=pltpu.VMEM)] * len(args)
    if scalars:
        specs[0] = pl.BlockSpec(memory_space=pltpu.SMEM)
    return pl.pallas_call(
        kernel,
        in_specs=specs,
        out_shape=[jax.ShapeDtypeStruct(s, f32) for s in outs],
        scratch_shapes=[pltpu.VMEM(s, f32) for s in scratch],
        compiler_params=pltpu.CompilerParams(vmem_limit_bytes=VMEM_BYTES),
        cost_estimate=pl.CostEstimate(flops=flops, bytes_accessed=1_000_000, transcendentals=0),
    )(*args)


def swapped(axis, one, two):
    size = lax.axis_size(axis)
    inner = [(i, i ^ 1) for i in range(size)]
    outer = []
    for i in range(1, size - 1, 2):
        outer += [(i, i + 1), (i + 1, i)]
    two = lax.ppermute(two, axis, outer)
    one = lax.ppermute(one, axis, inner)
    return one, two


def halos(axis, low, high):
    even = lax.axis_index(axis) % 2 == 0
    one, two = swapped(axis, jnp.where(even, high, low), jnp.where(even, low, high))
    return jnp.where(even, two, one), jnp.where(even, one, two)


def partner(x, mask):
    sizes = [lax.axis_size("gx"), lax.axis_size("gy")]
    pairs = []
    for i in range(sizes[0] * sizes[1]):
        gx, gy = divmod(i, sizes[1])
        pairs.append((i, (gx ^ mask[0]) * sizes[1] + (gy ^ mask[1])))
    return lax.ppermute(x, ("gx", "gy"), pairs)


CORE, X_NEAR, X_FAR, Y_NEAR, Y_FAR = (0, 1), (0, 2), (0, 6), (1, 0), (3, 0)
Z_ONE, Z_TWO, Z_FAR = (4, 0), (8, 0), (12, 8)


def second_half(step):
    gx, gy = lax.axis_index("gx"), lax.axis_index("gy")
    if step == CORE:
        return gy % 2 == 1
    if step == X_NEAR:
        return (gy // 2 + gy // 4) % 2 == 1
    return (gx + gx // 2) % 2 == 1


def half_sum(x, step):
    rows = x.shape[0] // 2
    upper = second_half(step)
    first, second = x[:rows], x[rows:]
    return jnp.where(upper, second, first) + partner(jnp.where(upper, first, second), step)


def in_order(mine, other, step):
    upper = second_half(step)
    return jnp.concatenate([jnp.where(upper, other, mine), jnp.where(upper, mine, other)], axis=0)


def tied(x, *others):
    return lax.optimization_barrier((x, *others))


def pair_sum(coarse, fine, step):
    both = jnp.concatenate([coarse, fine], axis=0)
    both = both + partner(both, step)
    return both[: coarse.shape[0]], both[coarse.shape[0] :]


def pair_whole(coarse, fine, step):
    other = partner(jnp.concatenate([coarse, fine], axis=0), step)
    return in_order(coarse, other[: coarse.shape[0]], step), fine + other[coarse.shape[0] :]


def local(
    coarse_out,
    coarse_cot,
    fine_conv,
    fine_bias_in,
    fine_proj,
    fine_bias_out,
    coarse_conv,
    coarse_bias_in,
    coarse_proj,
    coarse_bias_out,
):
    channels, nx, ny, nz = coarse_out.shape
    k = channels // 2
    h = coarse_conv.shape[1]
    fk, fh = fine_conv.shape[2], fine_conv.shape[1]
    size_x, size_y = lax.axis_size("gx"), lax.axis_size("gy")
    factor = float(4 * nx * ny * nz * size_x * size_y) ** -0.5
    at = jnp.stack([lax.axis_index("gx"), lax.axis_index("gy")]).astype(jnp.int32)
    c_conv, f_conv = jnp.transpose(coarse_conv, (0, 2, 1)), jnp.transpose(fine_conv, (0, 2, 1))

    u, one, two = call(
        ends_kernel, [(nx, ny, k, nz), (nx, 2, k, nz), (nx, 2, k, nz)], [], 500_000_000, at, coarse_out, scalars=True
    )
    u_y = swapped("gy", one, two)
    vd, cot_u, one, two = call(
        ends_vd_kernel,
        [(nx, ny, 2 * k, nz), (nx, ny, k, nz), (nx, 1, 2 * k, nz), (nx, 1, 2 * k, nz)],
        [],
        500_000_000,
        at,
        coarse_out,
        coarse_cot,
        scalars=True,
    )
    vd_y = swapped("gy", one, two)
    u_x = swapped("gx", *call(sides_kernel, [(2, ny + 4, k, nz)] * 2, [], 500_000_000, at, u, *u_y, scalars=True))
    inner, pre_in, wp, b_in = call(
        conv_inner_kernel,
        [(nx, 3 * k, (ny + 4) * nz), (nx - 2, h, (ny + 2) * nz), (3 * h, 27 * k), (h, 1)],
        [],
        2_500_000_000,
        at,
        u,
        *u_y,
        c_conv,
        coarse_bias_in[None, :],
        scalars=True,
    )
    vd_x = swapped("gx", *call(sides_kernel, [(1, ny + 2, 2 * k, nz)] * 2, [], 500_000_000, at, vd, *vd_y, scalars=True))
    outer, pre_out = call(
        conv_outer_kernel,
        [(4, 3 * k, (ny + 4) * nz), (4, h, (ny + 2) * nz)],
        [],
        4_000_000_000,
        at,
        inner,
        *u_x,
        wp,
        b_in,
        scalars=True,
    )
    q, c_gpre, low, coarse_grads = call(
        lambda *refs: coarse_kernel(factor, size_x, size_y, *refs),
        [(nx + 2, ny + 2, 2 * k, nz), (nx + 2, h, (ny + 2) * nz), (nx, k, ny * nz), (16 * k, 128)],
        [
            (nx, h, ny * nz),
            (nx, 2 * k, ny * nz),
            (9 * k + 16 + 2 * k, 4 * h),
            (9 * k + 2 * k, 4 * h),
            (2 * k, 128),
        ],
        6_000_000_000,
        at,
        inner,
        outer,
        pre_in,
        pre_out,
        vd,
        *vd_y,
        *vd_x,
        coarse_proj,
        coarse_bias_out[None, :],
        scalars=True,
    )
    coarse_grads = half_sum(coarse_grads, CORE)
    (dq,) = call(coarse_back_kernel, [(nx, ny, 2 * k, nz)], [], 2_500_000_000, c_gpre, low, cot_u, c_conv)
    coarse_grads, q, dq = tied(coarse_grads, q, dq)
    coarse_grads = half_sum(coarse_grads, Y_NEAR)

    fx, fy = 2 * nx, 2 * ny
    weights = (f_conv, fine_bias_in[None, :], fine_proj, fine_bias_out[None, :])
    sums_shapes = [(9 * fk + 16 + 2 * fk, 4 * fh), (9 * fk + 2 * fk, 4 * fh), (2 * fk, 128)]

    def fine(first, count, rows, last, *before):
        ins = (q, dq, *weights, *before)
        outs = [(rows, fy, 2 * fk, nz), (rows, fy, 2 * fk, nz), (rows, fy, fh, nz), *last]
        scratch = [(count + 2, 3 * fk, (fy + 2) * nz), (count, fk, fy * nz), (count, 2 * fk, fy * nz)]
        return call(
            lambda *refs: fine_kernel(factor, first, count, len(ins), len(outs), *refs),
            outs,
            scratch + (sums_shapes if before else []),
            4_500_000_000,
            *ins,
        )

    part = fine(0, nx, nx, sums_shapes)
    coarse_grads, *part = tied(coarse_grads, *part)
    coarse_grads = half_sum(coarse_grads, X_NEAR)
    field, cot, gpre, fine_grads = fine(nx, nx, fx, [(10 * fk, 128)], *part)
    coarse_grads, fine_grads = tied(coarse_grads, fine_grads)
    fine_grads = half_sum(fine_grads, CORE)

    def far(coarse, fine, steps):
        for step in steps:
            if step[0] < size_x and step[1] < size_y:
                coarse, fine = pair_sum(coarse, fine, step)
        return coarse, fine

    sums = far(coarse_grads, fine_grads, [X_FAR, Y_FAR])
    sums, gpre = tied(sums, gpre)
    cot, columns, rows = call(
        fine_back_kernel,
        [cot.shape, (2, fx + 2, fk, nz), (2, fy, fk, nz)],
        [(fx + 4, fh, fy * nz)],
        4_000_000_000,
        gpre,
        cot,
        f_conv,
    )
    sums = far(*sums, [Z_TWO, Z_ONE])
    sums, columns = tied(sums, columns)
    low, high = halos("gy", columns[0], columns[1])
    rows = jnp.concatenate([rows[:, :1] + low[:: fx + 1, None], rows[:, 1:-1], rows[:, -1:] + high[:: fx + 1, None]], axis=1)
    sums = far(*sums, [Z_FAR])
    sums, rows = tied(sums, rows)
    below, above = halos("gx", rows[0], rows[1])
    du = cot[:, :, :fk]
    du = jnp.concatenate([du[:, :1] + low[1:-1, None], du[:, 1:-1], du[:, -1:] + high[1:-1, None]], axis=1)
    du = jnp.concatenate([du[:1] + below[None], du[1:-1], du[-1:] + above[None]], axis=0)
    cot = jnp.concatenate([du, cot[:, :, fk:]], axis=2)

    coarse_grads, fine_grads = pair_whole(*pair_whole(*sums, X_NEAR), Y_NEAR)
    other = partner(jnp.concatenate([coarse_grads, fine_grads], axis=0), CORE)
    cut = coarse_grads.shape[0]
    sums = (coarse_grads, other[:cut], fine_grads, other[cut:])

    grads = call(
        unpack_kernel,
        [(27, fk, fh), (1, fh), (2 * fk, fh), (1, 2 * fk), (27, k, h), (1, h), (2 * k, h), (1, 2 * k)],
        [(16 * k, 128), (10 * fk, 128)],
        1_000_000,
        at,
        *sums,
        scalars=True,
    )
    f_conv, f_in, f_proj, f_out, c_conv, c_in, c_proj, c_out = grads
    return (
        jnp.transpose(field, (2, 0, 1, 3)),
        jnp.transpose(cot, (2, 0, 1, 3)),
        jnp.transpose(f_conv, (0, 2, 1)),
        f_in[0],
        f_proj,
        f_out[0],
        jnp.transpose(c_conv, (0, 2, 1)),
        c_in[0],
        c_proj,
        c_out[0],
    )


def solution(mesh):
    split_field = P(None, "gx", "gy", None)
    return jax.shard_map(
        local,
        mesh=mesh,
        in_specs=(split_field, split_field) + (P(),) * 8,
        out_specs=(split_field, split_field) + (P(),) * 8,
        check_vma=False,
    )
```

```python
import jax
import jax.numpy as jnp
from jax import lax
from jax.experimental import pallas as pl
from jax.experimental.pallas import tpu as pltpu
from jax.sharding import PartitionSpec as P

f32 = jnp.float32
bf16 = jnp.bfloat16
VMEM_BYTES = 24 * 1024 * 1024


def dot(a, b):
    return lax.dot_general(a, b, (((1,), (0,)), ((), ())), preferred_element_type=f32)


def dot_cells(a, b):
    return lax.dot_general(a, b, (((1,), (1,)), ((), ())), preferred_element_type=f32)


def split(x):
    top = x.astype(bf16).astype(f32)
    return top, x - top


def stacked(x, spare=0):
    top, rest = split(x)
    rows = [top, rest, top]
    if spare:
        rows.append(jnp.zeros((spare, x.shape[1]), f32))
    return jnp.concatenate(rows, axis=0).astype(bf16)


def thrice(x):
    top, rest = split(x)
    return jnp.concatenate([top, top, rest], axis=0)


def row_of(ref, x, first, count):
    return jnp.concatenate([ref[x, first + y] for y in range(count)], axis=1)


def shifted(x, step):
    lane = lax.broadcasted_iota(jnp.int32, (x.shape[0], 128), 1)
    edge = 0 if step > 0 else 127
    out = []
    for k in range(x.shape[1] // 128):
        moved = pltpu.roll(x[:, 128 * k : 128 * (k + 1)], step % 128, 1)
        out.append(jnp.where(lane == edge, 0.0, moved))
    return jnp.concatenate(out, axis=1)


def taps_along_z(x):
    return jnp.concatenate([shifted(x, 1), x, shifted(x, -1)], axis=0)


def window(o, rows, width, backward):
    parts = []
    for b in range(3):
        at = (2 - b if backward else b) * 128
        parts.append(o[b * rows : (b + 1) * rows, at : at + width])
    return parts[0] + parts[1] + parts[2]


def coupling(pre, v, dv, pj, pt, bo):
    half = v.shape[0]
    sig = jax.nn.sigmoid(pre)
    act = pre * sig
    out = dot(pj, stacked(act)) + bo
    sc = jnp.tanh(out[:half])
    centred = v - out[half:]
    lower = centred * jnp.exp(-sc)
    lower_cot = dv * jnp.exp(sc)
    g = jnp.concatenate([dv * centred * (1.0 - sc * sc), dv], axis=0)
    ga = dot(pt, stacked(g))
    gpre = ga * sig * (1.0 + pre * (1.0 - sig))
    return act, g, gpre, lower, lower_cot


def placed_at(x, before, after):
    rows = x.shape[0]
    parts = []
    if before:
        parts.append(jnp.zeros((rows, 128 * before), f32))
    parts.append(x)
    if after:
        parts.append(jnp.zeros((rows, 128 * after), f32))
    return jnp.concatenate(parts, axis=1) if len(parts) > 1 else x


def weight_products(patch, gpre, act, g):
    tops, rests = [], []
    for piece in [placed_at(gpre, b, 2 - b) for b in range(3)] + [placed_at(act, 1, 1)]:
        top, rest = split(piece)
        tops.append(top)
        rests.append(rest)
    right = jnp.concatenate(tops + rests, axis=0).astype(bf16)
    p_top, p_rest = split(patch)
    g_top, g_rest = split(placed_at(g, 1, 1))
    ones = jnp.ones((16, patch.shape[1]), f32)
    first = jnp.concatenate([p_top, ones, g_top], axis=0).astype(bf16)
    second = jnp.concatenate([p_rest, g_rest], axis=0).astype(bf16)
    wide = right.shape[0] // 2
    if wide < 256:
        both = dot_cells(jnp.concatenate([first, second], axis=0), right)
        a, b = both[: first.shape[0]], both[first.shape[0] :, :wide]
    else:
        a, b = dot_cells(first, right), dot_cells(second, right[:wide])
    return a[:, :wide] + a[:, wide:], b


def lane_sum(x):
    total = x[:, :128]
    for k in range(1, x.shape[1] // 128):
        total = total + x[:, 128 * k : 128 * (k + 1)]
    return total


def gathered(first, second, g_sum, taps, outs, lane_of_outs):
    conv = first[:taps] + second[:taps]
    bias_in = first[taps : taps + 8]
    proj = first[taps + 16 :] + second[taps:]
    total = jnp.broadcast_to(jnp.sum(g_sum, axis=1, keepdims=True), (outs, 128))
    row = lax.broadcasted_iota(jnp.int32, (outs, 128), 0)
    lane = lax.broadcasted_iota(jnp.int32, (outs, 128), 1)
    bias_out = jnp.sum(jnp.where(lane == row + lane_of_outs, total, 0.0), axis=0, keepdims=True)
    return conv, bias_in, proj, jnp.broadcast_to(bias_out, (8, 128))


def lanes_from(at, upper, lower):
    lane = lax.broadcasted_iota(jnp.int32, upper.shape, 1)
    return jnp.where(lane >= at, upper, lower)


def column(row):
    n = row.shape[1]
    i = lax.broadcasted_iota(jnp.int32, (n, n), 0)
    j = lax.broadcasted_iota(jnp.int32, (n, n), 1)
    return jnp.sum(jnp.where(i == j, jnp.broadcast_to(row, (n, n)), 0.0), axis=1, keepdims=True)


def forward_weight(conv_ref, spare):
    h = conv_ref.shape[2]
    parts = []
    for b in range(3):
        w = jnp.concatenate([conv_ref[9 * a + 3 * b + c] for a in range(3) for c in range(3)], axis=0)
        rows = thrice(w)
        if spare:
            rows = jnp.concatenate([rows, jnp.zeros((spare, h), f32)], axis=0)
        parts.append(rows.T)
    return jnp.concatenate(parts, axis=0).astype(bf16)


def back_weight(conv_ref):
    w = [jnp.concatenate([conv_ref[9 * a + t] for t in range(9)], axis=0).T for a in range(3)]
    return thrice(jnp.concatenate(w, axis=0)).T.astype(bf16)


def projections(proj_ref):
    p = proj_ref[...]
    return thrice(p.T).T.astype(bf16), thrice(p).T.astype(bf16)


def transposed_block(ref, first, last, x):
    return jnp.swapaxes(ref[first:last, x], 0, 1)


def ends_kernel(at_ref, w_ref, u_ref, one_ref, two_ref):
    nx, ny, k = u_ref.shape[0], u_ref.shape[1], u_ref.shape[2]
    even = at_ref[1] % 2 == 0
    for x in range(nx):
        u = transposed_block(w_ref, 0, k, x)
        u_ref[x] = u
        low, high = u[:2], u[ny - 2 :]
        one_ref[x] = lax.select(even, high, low)
        two_ref[x] = lax.select(even, low, high)


def ends_vd_kernel(at_ref, w_ref, dw_ref, vd_ref, cot_ref, one_ref, two_ref):
    nx, ny, k = cot_ref.shape[0], cot_ref.shape[1], cot_ref.shape[2]
    even = at_ref[1] % 2 == 0
    for x in range(nx):
        cot_ref[x] = transposed_block(dw_ref, 0, k, x)
        vd = jnp.concatenate([transposed_block(w_ref, k, 2 * k, x), transposed_block(dw_ref, k, 2 * k, x)], axis=1)
        vd_ref[x] = vd
        low, high = vd[:1], vd[ny - 1 :]
        one_ref[x] = lax.select(even, high, low)
        two_ref[x] = lax.select(even, low, high)


def sides_kernel(at_ref, f_ref, ya_ref, yb_ref, one_ref, two_ref):
    nx, rows = f_ref.shape[0], one_ref.shape[0]
    even_x, even_y = at_ref[0] % 2 == 0, at_ref[1] % 2 == 0

    def widened(x):
        a, b = ya_ref[x], yb_ref[x]
        return jnp.concatenate([lax.select(even_y, b, a), f_ref[x], lax.select(even_y, a, b)], axis=0)

    for x in range(rows):
        low, high = widened(x), widened(nx - rows + x)
        one_ref[x] = lax.select(even_x, high, low)
        two_ref[x] = lax.select(even_x, low, high)


def conv_inner_kernel(at_ref, u_ref, ya_ref, yb_ref, conv_ref, in_ref, taps_ref, pre_ref, wp_ref, bi_ref):
    nx, ny, k = u_ref.shape[0], u_ref.shape[1], u_ref.shape[2]
    h = conv_ref.shape[2]
    wp = forward_weight(conv_ref, 0)
    wp_ref[...] = wp.astype(f32)
    bi = column(in_ref[...])
    bi_ref[...] = bi
    even_y = at_ref[1] % 2 == 0
    taps = []
    for x in range(nx):
        a, b = row_of(ya_ref, x, 0, 2), row_of(yb_ref, x, 0, 2)
        low, high = lax.select(even_y, b, a), lax.select(even_y, a, b)
        taps_ref[x] = taps_along_z(jnp.concatenate([low, row_of(u_ref, x, 0, ny), high], axis=1))
    for x in range(nx - 2):
        patch = jnp.concatenate([taps_ref[x], taps_ref[x + 1], taps_ref[x + 2]], axis=0)
        pre_ref[x] = window(dot(wp, stacked(patch)), h, (ny + 2) * 128, False) + bi


def conv_outer_kernel(at_ref, inner_ref, xa_ref, xb_ref, wp_ref, bi_ref, taps_ref, pre_ref):
    nx, columns = inner_ref.shape[0], xa_ref.shape[1]
    h = bi_ref.shape[0]
    wp = wp_ref[...].astype(bf16)
    even_x = at_ref[0] % 2 == 0
    for x in range(2):
        a, b = row_of(xa_ref, x, 0, columns), row_of(xb_ref, x, 0, columns)
        taps_ref[x] = taps_along_z(lax.select(even_x, b, a))
        taps_ref[x + 2] = taps_along_z(lax.select(even_x, a, b))
    rows = [taps_ref[0], taps_ref[1], inner_ref[0], inner_ref[1], inner_ref[nx - 2], inner_ref[nx - 1], taps_ref[2], taps_ref[3]]
    for i, at in enumerate((0, 1, 4, 5)):
        patch = jnp.concatenate(rows[at : at + 3], axis=0)
        pre_ref[i] = window(dot(wp, stacked(patch)), h, (columns - 2) * 128, False) + bi_ref[...]


def coarse_kernel(factor, size_x, size_y, at_ref, inner_ref, outer_ref, pre_in_ref, pre_out_ref, vd_ref, ya_ref, yb_ref, xa_ref, xb_ref,
                  proj_ref, out_ref, q_ref, gpre_ref, low_ref, grads_ref,
                  act_s, g_s, sums, rests, g_sum):
    nx, ny, k = vd_ref.shape[0], vd_ref.shape[1], vd_ref.shape[2] // 2
    wide, own = (ny + 2) * 128, slice(128, 128 * (ny + 1))
    pj, pt = projections(proj_ref)
    bo = column(out_ref[...])
    even_x, even_y = at_ref[0] % 2 == 0, at_ref[1] % 2 == 0
    taps = [(outer_ref, 0), (outer_ref, 1)] + [(inner_ref, x) for x in range(nx)] + [(outer_ref, 2), (outer_ref, 3)]
    pres = [(pre_out_ref, 0), (pre_out_ref, 1)] + [(pre_in_ref, x) for x in range(nx - 2)] + [(pre_out_ref, 2), (pre_out_ref, 3)]
    low_x = jnp.where(at_ref[0] == 0, 0.0, 1.0)
    high_x = jnp.where(at_ref[0] == size_x - 1, 0.0, 1.0)
    low_y = jnp.where(at_ref[1] == 0, 0.0, 1.0)
    high_y = jnp.where(at_ref[1] == size_y - 1, 0.0, 1.0)

    def forward(x, vd, inside):
        pre_ref, at = pres[x]
        act, g, gpre, lower, lower_cot = coupling(pre_ref[at], vd[:k], vd[k:], pj, pt, bo)
        taps_ref, at = taps[x + 1]
        u = taps_ref[at][k : 2 * k, 128 : 128 + wide]
        for y in range(ny + 2):
            cols = slice(128 * y, 128 * (y + 1))
            here = inside * (low_y if y == 0 else high_y if y == ny + 1 else 1.0)
            q_ref[x, y, :k] = u[:, cols]
            q_ref[x, y, k:] = lower[:, cols] * here
        gpre_ref[x] = gpre
        return act, g, lower_cot

    sums[...] = jnp.zeros_like(sums)
    rests[...] = jnp.zeros_like(rests)
    g_sum[...] = jnp.zeros_like(g_sum)

    for x in range(nx):
        a, b = ya_ref[x, 0], yb_ref[x, 0]
        vd = jnp.concatenate([lax.select(even_y, b, a), row_of(vd_ref, x, 0, ny), lax.select(even_y, a, b)], axis=1)
        act, g, lower_cot = forward(x + 1, vd, 1.0)
        low_ref[x] = lower_cot[:, own]
        act_s[x] = act[:, own]
        g_s[x] = g[:, own]
    a, b = row_of(xa_ref, 0, 0, ny + 2), row_of(xb_ref, 0, 0, ny + 2)
    forward(0, lax.select(even_x, b, a), low_x)
    forward(nx + 1, lax.select(even_x, a, b), high_x)

    for x in range(nx):
        patch = jnp.concatenate([ref[at][:, 128 : 128 + wide] for ref, at in taps[x + 1 : x + 4]], axis=0)
        a, b = weight_products(patch, gpre_ref[x + 1][:, own], act_s[x], g_s[x])
        sums[...] += a
        rests[...] += b
        g_sum[...] += lane_sum(g_s[x])
    rows, fold = 9 * k, 9 * k // 2
    conv, bias_in, proj, bias_out = gathered(sums[...], rests[...], g_sum[...], rows, 2 * k, 64)
    grads_ref[:rows] = conv[:, :128] * factor
    second = conv[:, 128:] * factor
    grads_ref[rows : rows + fold] = lanes_from(64, pltpu.roll(second[fold:], 64, 1), second[:fold])
    proj = proj[:, 128:] * factor
    at = rows + fold
    grads_ref[at : at + k] = lanes_from(64, proj[k:], pltpu.roll(proj[:k], 64, 1))
    grads_ref[at + k : at + k + 8] = lanes_from(64, bias_out, bias_in[:, :128]) * factor
    grads_ref[at + k + 8 :] = jnp.zeros((grads_ref.shape[0] - at - k - 8, 128), f32)


def coarse_back_kernel(gpre_ref, low_ref, cot_ref, conv_ref, dq_ref):
    nx, ny, k = low_ref.shape[0], cot_ref.shape[1], low_ref.shape[1]
    wd = back_weight(conv_ref)

    def back(x, _):
        parts = jnp.concatenate([gpre_ref[x + 2], gpre_ref[x + 1], gpre_ref[x]], axis=0)
        s = window(dot(wd, stacked(parts)), 3 * k, ny * 128, True)
        du = s[k : 2 * k] + shifted(s[:k], -1) + shifted(s[2 * k :], 1)
        low = low_ref[x]
        for y in range(ny):
            cols = slice(128 * y, 128 * (y + 1))
            dq_ref[x, y, :k] = cot_ref[x, y] + du[:, cols]
            dq_ref[x, y, k:] = low[:, cols]
        return 0

    lax.fori_loop(0, nx, back, 0, unroll=True)


def finer_rows(field):
    c = field.shape[0] // 4
    a, b, d, e = [field[i * c : (i + 1) * c] for i in range(4)]
    sum_u, sum_l, dif_u, dif_l = a + b, d + e, a - b, d - e
    rows = []
    for p, q in ((sum_u, sum_l), (dif_u, dif_l)):
        even, odd = 0.5 * (p + q), 0.5 * (p - q)
        cols = []
        for k in range(even.shape[1] // 128):
            cols += [even[:, 128 * k : 128 * (k + 1)], odd[:, 128 * k : 128 * (k + 1)]]
        rows.append(jnp.concatenate(cols, axis=1))
    return rows


def fine_kernel(factor, first, count, n_in, n_out, *refs):
    q_ref, dq_ref, conv_ref, in_ref, proj_ref, out_ref = refs[:6]
    before = refs[6:n_in]
    field_ref, cot_ref, gpre_ref, *grads_ref = refs[n_in : n_in + n_out]
    scratch = refs[n_in + n_out :]
    taps, v_s, dz_s = scratch[:3]
    sums, rests, g_sum = scratch[3:] if before else grads_ref
    ny = field_ref.shape[1]
    k = field_ref.shape[2] // 2
    h = conv_ref.shape[2]
    wp = forward_weight(conv_ref, 8)
    pj, pt = projections(proj_ref)
    bi, bo = column(in_ref[...]), column(out_ref[...])
    cy = ny // 2

    for x in range(q_ref.shape[0]):
        wanted = [r for r in (2 * x, 2 * x + 1) if first + 1 <= r <= first + count + 2]
        if wanted:
            pair = finer_rows(row_of(q_ref, x, 0, cy + 2))
        for r in wanted:
            z = pair[r - 2 * x]
            taps[r - 1 - first] = taps_along_z(z[:k, 128 : 128 * (ny + 3)])
            if first + 2 <= r < first + count + 2:
                v_s[r - 2 - first] = z[k:, 256 : 128 * (ny + 2)]
    for x in range(first // 2, (first + count) // 2):
        pair = finer_rows(row_of(dq_ref, x, 0, cy))
        dz_s[2 * x - first] = pair[0]
        dz_s[2 * x + 1 - first] = pair[1]

    if before:
        sums[...], rests[...], g_sum[...] = before[3][...], before[4][...], before[5][...]
        for ref, old in zip((field_ref, cot_ref, gpre_ref), before):
            ref[:first] = old[...]
    else:
        sums[...] = jnp.zeros_like(sums)
        rests[...] = jnp.zeros_like(rests)
        g_sum[...] = jnp.zeros_like(g_sum)
    at = first if before else 0

    for x in range(count):
        patch = jnp.concatenate([taps[x], taps[x + 1], taps[x + 2]], axis=0)
        pre = window(dot(wp, stacked(patch, 8)), h, ny * 128, False) + bi
        dz = dz_s[x]
        act, g, gpre, lower, lower_cot = coupling(pre, v_s[x], dz[k:], pj, pt, bo)
        a, b = weight_products(patch, gpre, act, g)
        sums[...] += a
        rests[...] += b
        g_sum[...] += lane_sum(g)
        field = jnp.concatenate([taps[x + 1][k : 2 * k, 128 : 128 * (ny + 1)], lower], axis=0)
        cot = jnp.concatenate([dz[:k], lower_cot], axis=0)
        for y in range(ny):
            cols = slice(128 * y, 128 * (y + 1))
            field_ref[at + x, y] = field[:, cols]
            cot_ref[at + x, y] = cot[:, cols]
            gpre_ref[at + x, y] = gpre[:, cols]

    if before:
        (grads,) = grads_ref
        conv, bias_in, proj, bias_out = gathered(sums[...], rests[...], g_sum[...], 9 * k, 2 * k, 3 * h)
        spare = jnp.zeros((9 * k - 2 * k - 16, 128), f32)
        others = jnp.concatenate([proj, pltpu.roll(bias_in, h, 1), bias_out, spare], axis=0)
        grads[: 9 * k] = lanes_from(3 * h, others, conv) * factor
        grads[9 * k :] = jnp.zeros((grads.shape[0] - 9 * k, 128), f32)


def fine_back_kernel(gpre_ref, cot_ref, conv_ref, out_ref, columns_ref, rows_ref, gpre_s):
    nx, ny = cot_ref.shape[0], cot_ref.shape[1]
    k = cot_ref.shape[2] // 2
    h = gpre_ref.shape[2]
    wd = back_weight(conv_ref)
    for x in (0, 1, nx + 2, nx + 3):
        gpre_s[x] = jnp.zeros((h, ny * 128), f32)

    def fill(x, _):
        gpre_s[x + 2] = row_of(gpre_ref, x, 0, ny)
        return 0

    lax.fori_loop(0, nx, fill, 0, unroll=True)

    def contributions(x):
        parts = jnp.concatenate([gpre_s[x + 2], gpre_s[x + 1], gpre_s[x]], axis=0)
        o = dot(wd, stacked(parts))
        s = [placed_at(o[b * 3 * k : (b + 1) * 3 * k], b, 2 - b) for b in range(3)]
        s = s[0] + s[1] + s[2]
        du = s[k : 2 * k] + shifted(s[:k], -1) + shifted(s[2 * k :], 1)
        columns_ref[0, x] = du[:, :128]
        columns_ref[1, x] = du[:, 128 * (ny + 1) :]
        return du

    def inner(x, _):
        du = contributions(x + 1)
        for y in range(ny):
            out_ref[x, y, :k] = cot_ref[x, y, :k] + du[:, 128 * (y + 1) : 128 * (y + 2)]
            out_ref[x, y, k:] = cot_ref[x, y, k:]
        return 0

    def outer(i, _):
        du = contributions(i * (nx + 1))
        for y in range(ny):
            rows_ref[i, y] = du[:, 128 * (y + 1) : 128 * (y + 2)]
        return 0

    lax.fori_loop(0, nx, inner, 0, unroll=True)
    lax.fori_loop(0, 2, outer, 0, unroll=True)


def corners_kernel(rows_ref, low_ref, high_ref, out_ref):
    count = out_ref.shape[1]
    for i, x in ((0, 0), (1, low_ref.shape[0] - 1)):
        for y in range(count):
            more = [ref[x] for ref, at in ((low_ref, 0), (high_ref, count - 1)) if at == y]
            out_ref[i, y] = sum(more, rows_ref[i, y])


def rims_kernel(cot_ref, low_ref, high_ref, below_ref, above_ref, out_ref):
    nx, ny, k = cot_ref.shape[0], cot_ref.shape[1], low_ref.shape[1]
    for x in range(nx):
        cells = []
        for y in range(ny):
            du = cot_ref[x, y, :k]
            for ref, at in ((low_ref, y == 0), (high_ref, y == ny - 1)):
                if at:
                    du = du + ref[x + 1]
            for ref, at in ((below_ref, x == 0), (above_ref, x == nx - 1)):
                if at:
                    du = du + ref[y]
            cells.append(jnp.concatenate([du, cot_ref[x, y, k:]], axis=0))
        out_ref[:, x] = jnp.swapaxes(jnp.stack(cells, axis=0), 0, 1)


def unpack_kernel(at_ref, coarse_ref, coarse_other, fine_ref, fine_other,
                  f_conv, f_in, f_proj, f_out, c_conv, c_in, c_proj, c_out, coarse, fine):
    first = at_ref[1] % 2 == 0
    for whole, mine, other in ((coarse, coarse_ref, coarse_other), (fine, fine_ref, fine_other)):
        rows = mine.shape[0]
        a, b = mine[...], other[...]
        whole[:rows] = lax.select(first, a, b)
        whole[rows:] = lax.select(first, b, a)

    k, h = c_conv.shape[1], c_conv.shape[2]
    rows, fold = 9 * k, 9 * k // 2
    ahead = coarse[:rows]
    second = coarse[rows : rows + fold]
    taps = [ahead, pltpu.roll(ahead, 64, 1), jnp.concatenate([second, pltpu.roll(second, 64, 1)], axis=0)]
    for t in range(27):
        a, b, c = t // 9, t // 3 % 3, t % 3
        c_conv[t] = taps[b][(3 * a + c) * k : (3 * a + c + 1) * k, :h]
    at = rows + fold
    proj = coarse[at : at + k]
    c_proj[:k] = proj[:, :h]
    c_proj[k:] = pltpu.roll(proj, 64, 1)[:, :h]
    biases = coarse[at + k : at + k + 8]
    c_in[...] = biases[:1, :h]
    c_out[...] = pltpu.roll(biases, 64, 1)[:1, : 2 * k]

    k, h = f_conv.shape[1], f_conv.shape[2]
    whole = fine[: 9 * k]
    parts = [whole] + [pltpu.roll(whole, 128 - b * h, 1) for b in (1, 2, 3)]
    for t in range(27):
        a, b, c = t // 9, t // 3 % 3, t % 3
        f_conv[t] = parts[b][(3 * a + c) * k : (3 * a + c + 1) * k, :h]
    f_proj[...] = parts[3][: 2 * k, :h]
    f_in[...] = parts[3][2 * k : 2 * k + 1, :h]
    f_out[...] = parts[3][2 * k + 8 : 2 * k + 9, : 2 * k]


def call(kernel, outs, scratch, flops, *args, scalars=False):
    specs = [pl.BlockSpec(memory_space=pltpu.VMEM)] * len(args)
    if scalars:
        specs[0] = pl.BlockSpec(memory_space=pltpu.SMEM)
    return pl.pallas_call(
        kernel,
        in_specs=specs,
        out_shape=[jax.ShapeDtypeStruct(s, f32) for s in outs],
        scratch_shapes=[pltpu.VMEM(s, f32) for s in scratch],
        compiler_params=pltpu.CompilerParams(vmem_limit_bytes=VMEM_BYTES),
        cost_estimate=pl.CostEstimate(flops=flops, bytes_accessed=1_000_000, transcendentals=0),
    )(*args)


def swapped(axis, one, two):
    size = lax.axis_size(axis)
    inner = [(i, i ^ 1) for i in range(size)]
    outer = []
    for i in range(1, size - 1, 2):
        outer += [(i, i + 1), (i + 1, i)]
    two = lax.ppermute(two, axis, outer)
    one = lax.ppermute(one, axis, inner)
    return one, two


def halos(axis, low, high):
    even = lax.axis_index(axis) % 2 == 0
    one, two = swapped(axis, jnp.where(even, high, low), jnp.where(even, low, high))
    return jnp.where(even, two, one), jnp.where(even, one, two)


def partner(x, mask):
    sizes = [lax.axis_size("gx"), lax.axis_size("gy")]
    pairs = []
    for i in range(sizes[0] * sizes[1]):
        gx, gy = divmod(i, sizes[1])
        to = (gx ^ mask[0], gy ^ mask[1])
        if to[0] < sizes[0] and to[1] < sizes[1]:
            pairs.append((i, to[0] * sizes[1] + to[1]))
    return lax.ppermute(x, ("gx", "gy"), pairs)


CORE, X_NEAR, X_FAR, Y_NEAR, Y_FAR = (0, 1), (0, 2), (0, 6), (1, 0), (3, 0)
Z_ONE, Z_TWO, Z_FAR = (4, 0), (8, 0), (12, 8)


def second_half(step):
    gx, gy = lax.axis_index("gx"), lax.axis_index("gy")
    if step == CORE:
        return gy % 2 == 1
    if step == X_NEAR:
        return (gy // 2 + gy // 4) % 2 == 1
    return (gx + gx // 2) % 2 == 1


def half_sum(x, step):
    rows = x.shape[0] // 2
    upper = second_half(step)
    first, second = x[:rows], x[rows:]
    return jnp.where(upper, second, first) + partner(jnp.where(upper, first, second), step)


def in_order(mine, other, step):
    upper = second_half(step)
    return jnp.concatenate([jnp.where(upper, other, mine), jnp.where(upper, mine, other)], axis=0)


def tied(x, *others):
    return lax.optimization_barrier((x, *others))


def partners(x, first, second):
    both = (first[0] ^ second[0], first[1] ^ second[1])
    return partner(x, first), partner(x, second), partner(x, both)


def four_sum(coarse, fine, first, second):
    both = jnp.concatenate([coarse, fine], axis=0)
    a, b, c = partners(both, first, second)
    both = (both + a) + (b + c)
    return both[: coarse.shape[0]], both[coarse.shape[0] :]


def pair_sum(coarse, fine, step):
    both = jnp.concatenate([coarse, fine], axis=0)
    both = both + partner(both, step)
    return both[: coarse.shape[0]], both[coarse.shape[0] :]


def four_whole(coarse, fine, first, second):
    cut = coarse.shape[0]
    a, b, c = partners(jnp.concatenate([coarse, fine], axis=0), first, second)
    mine, other = in_order(coarse, a[:cut], first), in_order(b[:cut], c[:cut], first)
    return in_order(mine, other, second), (fine + a[cut:]) + (b[cut:] + c[cut:])


def local(
    coarse_out,
    coarse_cot,
    fine_conv,
    fine_bias_in,
    fine_proj,
    fine_bias_out,
    coarse_conv,
    coarse_bias_in,
    coarse_proj,
    coarse_bias_out,
):
    channels, nx, ny, nz = coarse_out.shape
    k = channels // 2
    h = coarse_conv.shape[1]
    fk, fh = fine_conv.shape[2], fine_conv.shape[1]
    size_x, size_y = lax.axis_size("gx"), lax.axis_size("gy")
    factor = float(4 * nx * ny * nz * size_x * size_y) ** -0.5
    at = jnp.stack([lax.axis_index("gx"), lax.axis_index("gy")]).astype(jnp.int32)
    c_conv, f_conv = jnp.transpose(coarse_conv, (0, 2, 1)), jnp.transpose(fine_conv, (0, 2, 1))

    u, one, two = call(
        ends_kernel, [(nx, ny, k, nz), (nx, 2, k, nz), (nx, 2, k, nz)], [], 500_000_000, at, coarse_out, scalars=True
    )
    u_y = swapped("gy", one, two)
    vd, cot_u, one, two = call(
        ends_vd_kernel,
        [(nx, ny, 2 * k, nz), (nx, ny, k, nz), (nx, 1, 2 * k, nz), (nx, 1, 2 * k, nz)],
        [],
        500_000_000,
        at,
        coarse_out,
        coarse_cot,
        scalars=True,
    )
    vd_y = swapped("gy", one, two)
    u_x = swapped("gx", *call(sides_kernel, [(2, ny + 4, k, nz)] * 2, [], 500_000_000, at, u, *u_y, scalars=True))
    inner, pre_in, wp, b_in = call(
        conv_inner_kernel,
        [(nx, 3 * k, (ny + 4) * nz), (nx - 2, h, (ny + 2) * nz), (3 * h, 27 * k), (h, 1)],
        [],
        2_500_000_000,
        at,
        u,
        *u_y,
        c_conv,
        coarse_bias_in[None, :],
        scalars=True,
    )
    vd_x = swapped("gx", *call(sides_kernel, [(1, ny + 2, 2 * k, nz)] * 2, [], 500_000_000, at, vd, *vd_y, scalars=True))
    outer, pre_out = call(
        conv_outer_kernel,
        [(4, 3 * k, (ny + 4) * nz), (4, h, (ny + 2) * nz)],
        [],
        4_000_000_000,
        at,
        inner,
        *u_x,
        wp,
        b_in,
        scalars=True,
    )
    q, c_gpre, low, coarse_grads = call(
        lambda *refs: coarse_kernel(factor, size_x, size_y, *refs),
        [(nx + 2, ny + 2, 2 * k, nz), (nx + 2, h, (ny + 2) * nz), (nx, k, ny * nz), (16 * k, 128)],
        [
            (nx, h, ny * nz),
            (nx, 2 * k, ny * nz),
            (9 * k + 16 + 2 * k, 4 * h),
            (9 * k + 2 * k, 4 * h),
            (2 * k, 128),
        ],
        6_000_000_000,
        at,
        inner,
        outer,
        pre_in,
        pre_out,
        vd,
        *vd_y,
        *vd_x,
        coarse_proj,
        coarse_bias_out[None, :],
        scalars=True,
    )
    coarse_grads = half_sum(coarse_grads, CORE)
    (dq,) = call(coarse_back_kernel, [(nx, ny, 2 * k, nz)], [], 2_500_000_000, c_gpre, low, cot_u, c_conv)
    coarse_grads, q, dq = tied(coarse_grads, q, dq)
    coarse_grads = half_sum(coarse_grads, Y_NEAR)

    fx, fy = 2 * nx, 2 * ny
    weights = (f_conv, fine_bias_in[None, :], fine_proj, fine_bias_out[None, :])
    sums_shapes = [(9 * fk + 16 + 2 * fk, 4 * fh), (9 * fk + 2 * fk, 4 * fh), (2 * fk, 128)]

    def fine(first, count, rows, last, *before):
        ins = (q, dq, *weights, *before)
        outs = [(rows, fy, 2 * fk, nz), (rows, fy, 2 * fk, nz), (rows, fy, fh, nz), *last]
        scratch = [(count + 2, 3 * fk, (fy + 2) * nz), (count, fk, fy * nz), (count, 2 * fk, fy * nz)]
        return call(
            lambda *refs: fine_kernel(factor, first, count, len(ins), len(outs), *refs),
            outs,
            scratch + (sums_shapes if before else []),
            4_500_000_000,
            *ins,
        )

    part = fine(0, nx, nx, sums_shapes)
    coarse_grads, *part = tied(coarse_grads, *part)
    coarse_grads = half_sum(coarse_grads, X_NEAR)
    field, cot, gpre, fine_grads = fine(nx, nx, fx, [(10 * fk, 128)], *part)
    coarse_grads, fine_grads = tied(coarse_grads, fine_grads)
    fine_grads = half_sum(fine_grads, CORE)

    sums = four_sum(coarse_grads, fine_grads, X_FAR, Y_FAR)
    sums, gpre = tied(sums, gpre)
    cot, columns, rows = call(
        fine_back_kernel,
        [cot.shape, (2, fx + 2, fk, nz), (2, fy, fk, nz)],
        [(fx + 4, fh, fy * nz)],
        4_000_000_000,
        gpre,
        cot,
        f_conv,
    )
    low, high = halos("gy", columns[0], columns[1])
    sums = four_sum(*sums, Z_ONE, Z_TWO)
    sums, low, high = tied(sums, low, high)
    (rows,) = call(corners_kernel, [rows.shape], [], 6_000_000_000, rows, low, high)
    below, above = halos("gx", rows[0], rows[1])
    sums = pair_sum(*sums, Z_FAR)
    (cot,) = call(rims_kernel, [(2 * fk, fx, fy, nz)], [], 2_000_000_000, cot, low, high, below, above)
    coarse_grads, fine_grads = four_whole(*sums, X_NEAR, Y_NEAR)
    other = partner(jnp.concatenate([coarse_grads, fine_grads], axis=0), CORE)
    cut = coarse_grads.shape[0]
    sums = (coarse_grads, other[:cut], fine_grads, other[cut:])

    grads = call(
        unpack_kernel,
        [(27, fk, fh), (1, fh), (2 * fk, fh), (1, 2 * fk), (27, k, h), (1, h), (2 * k, h), (1, 2 * k)],
        [(16 * k, 128), (10 * fk, 128)],
        1_000_000,
        at,
        *sums,
        scalars=True,
    )
    f_conv, f_in, f_proj, f_out, c_conv, c_in, c_proj, c_out = grads
    return (
        jnp.transpose(field, (2, 0, 1, 3)),
        cot,
        jnp.transpose(f_conv, (0, 2, 1)),
        f_in[0],
        f_proj,
        f_out[0],
        jnp.transpose(c_conv, (0, 2, 1)),
        c_in[0],
        c_proj,
        c_out[0],
    )


def solution(mesh):
    split_field = P(None, "gx", "gy", None)
    return jax.shard_map(
        local,
        mesh=mesh,
        in_specs=(split_field, split_field) + (P(),) * 8,
        out_specs=(split_field, split_field) + (P(),) * 8,
        check_vma=False,
    )
```

```python
import jax
import jax.numpy as jnp
from jax import lax
from jax.experimental import pallas as pl
from jax.experimental.pallas import tpu as pltpu
from jax.sharding import PartitionSpec as P

f32 = jnp.float32
bf16 = jnp.bfloat16
VMEM_BYTES = 24 * 1024 * 1024


def dot(a, b):
    return lax.dot_general(a, b, (((1,), (0,)), ((), ())), preferred_element_type=f32)


def dot_cells(a, b):
    return lax.dot_general(a, b, (((1,), (1,)), ((), ())), preferred_element_type=f32)


def split(x):
    top = x.astype(bf16).astype(f32)
    return top, x - top


def stacked(x, spare=0):
    top, rest = split(x)
    rows = [top, rest, top]
    if spare:
        rows.append(jnp.zeros((spare, x.shape[1]), f32))
    return jnp.concatenate(rows, axis=0).astype(bf16)


def thrice(x):
    top, rest = split(x)
    return jnp.concatenate([top, top, rest], axis=0)


def row_of(ref, x, first, count):
    return jnp.concatenate([ref[x, first + y] for y in range(count)], axis=1)


def shifted(x, step):
    lane = lax.broadcasted_iota(jnp.int32, (x.shape[0], 128), 1)
    edge = 0 if step > 0 else 127
    out = []
    for k in range(x.shape[1] // 128):
        moved = pltpu.roll(x[:, 128 * k : 128 * (k + 1)], step % 128, 1)
        out.append(jnp.where(lane == edge, 0.0, moved))
    return jnp.concatenate(out, axis=1)


def taps_along_z(x):
    return jnp.concatenate([shifted(x, 1), x, shifted(x, -1)], axis=0)


def window(o, rows, width, backward):
    parts = []
    for b in range(3):
        at = (2 - b if backward else b) * 128
        parts.append(o[b * rows : (b + 1) * rows, at : at + width])
    return parts[0] + parts[1] + parts[2]


def coupling(pre, v, dv, pj, pt, bo):
    half = v.shape[0]
    sig = jax.nn.sigmoid(pre)
    act = pre * sig
    out = dot(pj, stacked(act)) + bo
    sc = jnp.tanh(out[:half])
    centred = v - out[half:]
    lower = centred * jnp.exp(-sc)
    lower_cot = dv * jnp.exp(sc)
    g = jnp.concatenate([dv * centred * (1.0 - sc * sc), dv], axis=0)
    ga = dot(pt, stacked(g))
    gpre = ga * sig * (1.0 + pre * (1.0 - sig))
    return act, g, gpre, lower, lower_cot


def placed_at(x, before, after):
    rows = x.shape[0]
    parts = []
    if before:
        parts.append(jnp.zeros((rows, 128 * before), f32))
    parts.append(x)
    if after:
        parts.append(jnp.zeros((rows, 128 * after), f32))
    return jnp.concatenate(parts, axis=1) if len(parts) > 1 else x


def weight_products(patch, gpre, act, g):
    tops, rests = [], []
    for piece in [placed_at(gpre, b, 2 - b) for b in range(3)] + [placed_at(act, 1, 1)]:
        top, rest = split(piece)
        tops.append(top)
        rests.append(rest)
    right = jnp.concatenate(tops + rests, axis=0).astype(bf16)
    p_top, p_rest = split(patch)
    g_top, g_rest = split(placed_at(g, 1, 1))
    ones = jnp.ones((16, patch.shape[1]), f32)
    first = jnp.concatenate([p_top, ones, g_top], axis=0).astype(bf16)
    second = jnp.concatenate([p_rest, g_rest], axis=0).astype(bf16)
    wide = right.shape[0] // 2
    if wide < 256:
        both = dot_cells(jnp.concatenate([first, second], axis=0), right)
        a, b = both[: first.shape[0]], both[first.shape[0] :, :wide]
    else:
        a, b = dot_cells(first, right), dot_cells(second, right[:wide])
    return a[:, :wide] + a[:, wide:], b


def lane_sum(x):
    total = x[:, :128]
    for k in range(1, x.shape[1] // 128):
        total = total + x[:, 128 * k : 128 * (k + 1)]
    return total


def gathered(first, second, g_sum, taps, outs, lane_of_outs):
    conv = first[:taps] + second[:taps]
    bias_in = first[taps : taps + 8]
    proj = first[taps + 16 :] + second[taps:]
    total = jnp.broadcast_to(jnp.sum(g_sum, axis=1, keepdims=True), (outs, 128))
    row = lax.broadcasted_iota(jnp.int32, (outs, 128), 0)
    lane = lax.broadcasted_iota(jnp.int32, (outs, 128), 1)
    bias_out = jnp.sum(jnp.where(lane == row + lane_of_outs, total, 0.0), axis=0, keepdims=True)
    return conv, bias_in, proj, jnp.broadcast_to(bias_out, (8, 128))


def lanes_from(at, upper, lower):
    lane = lax.broadcasted_iota(jnp.int32, upper.shape, 1)
    return jnp.where(lane >= at, upper, lower)


def column(row):
    n = row.shape[1]
    i = lax.broadcasted_iota(jnp.int32, (n, n), 0)
    j = lax.broadcasted_iota(jnp.int32, (n, n), 1)
    return jnp.sum(jnp.where(i == j, jnp.broadcast_to(row, (n, n)), 0.0), axis=1, keepdims=True)


def forward_weight(conv_ref, spare):
    h = conv_ref.shape[2]
    parts = []
    for b in range(3):
        w = jnp.concatenate([conv_ref[9 * a + 3 * b + c] for a in range(3) for c in range(3)], axis=0)
        rows = thrice(w)
        if spare:
            rows = jnp.concatenate([rows, jnp.zeros((spare, h), f32)], axis=0)
        parts.append(rows.T)
    return jnp.concatenate(parts, axis=0).astype(bf16)


def back_weight(conv_ref):
    w = [jnp.concatenate([conv_ref[9 * a + t] for t in range(9)], axis=0).T for a in range(3)]
    return thrice(jnp.concatenate(w, axis=0)).T.astype(bf16)


def projections(proj_ref):
    p = proj_ref[...]
    return thrice(p.T).T.astype(bf16), thrice(p).T.astype(bf16)


def transposed_block(ref, first, last, x):
    return jnp.swapaxes(ref[first:last, x], 0, 1)


def ends_kernel(at_ref, w_ref, u_ref, one_ref, two_ref):
    nx, ny, k = u_ref.shape[0], u_ref.shape[1], u_ref.shape[2]
    even = at_ref[1] % 2 == 0
    for x in range(nx):
        u = transposed_block(w_ref, 0, k, x)
        u_ref[x] = u
        low, high = u[:2], u[ny - 2 :]
        one_ref[x] = lax.select(even, high, low)
        two_ref[x] = lax.select(even, low, high)


def ends_vd_kernel(at_ref, w_ref, dw_ref, vd_ref, cot_ref, one_ref, two_ref):
    nx, ny, k = cot_ref.shape[0], cot_ref.shape[1], cot_ref.shape[2]
    even = at_ref[1] % 2 == 0
    for x in range(nx):
        cot_ref[x] = transposed_block(dw_ref, 0, k, x)
        vd = jnp.concatenate([transposed_block(w_ref, k, 2 * k, x), transposed_block(dw_ref, k, 2 * k, x)], axis=1)
        vd_ref[x] = vd
        low, high = vd[:1], vd[ny - 1 :]
        one_ref[x] = lax.select(even, high, low)
        two_ref[x] = lax.select(even, low, high)


def sides_kernel(at_ref, f_ref, ya_ref, yb_ref, one_ref, two_ref):
    nx, rows = f_ref.shape[0], one_ref.shape[0]
    even_x, even_y = at_ref[0] % 2 == 0, at_ref[1] % 2 == 0

    def widened(x):
        a, b = ya_ref[x], yb_ref[x]
        return jnp.concatenate([lax.select(even_y, b, a), f_ref[x], lax.select(even_y, a, b)], axis=0)

    for x in range(rows):
        low, high = widened(x), widened(nx - rows + x)
        one_ref[x] = lax.select(even_x, high, low)
        two_ref[x] = lax.select(even_x, low, high)


def conv_inner_kernel(at_ref, u_ref, ya_ref, yb_ref, conv_ref, in_ref, taps_ref, pre_ref, wp_ref, bi_ref):
    nx, ny, k = u_ref.shape[0], u_ref.shape[1], u_ref.shape[2]
    h = conv_ref.shape[2]
    wp = forward_weight(conv_ref, 0)
    wp_ref[...] = wp.astype(f32)
    bi = column(in_ref[...])
    bi_ref[...] = bi
    even_y = at_ref[1] % 2 == 0
    taps = []
    for x in range(nx):
        a, b = row_of(ya_ref, x, 0, 2), row_of(yb_ref, x, 0, 2)
        low, high = lax.select(even_y, b, a), lax.select(even_y, a, b)
        taps_ref[x] = taps_along_z(jnp.concatenate([low, row_of(u_ref, x, 0, ny), high], axis=1))
    for x in range(nx - 2):
        patch = jnp.concatenate([taps_ref[x], taps_ref[x + 1], taps_ref[x + 2]], axis=0)
        pre_ref[x] = window(dot(wp, stacked(patch)), h, (ny + 2) * 128, False) + bi


def conv_outer_kernel(at_ref, inner_ref, xa_ref, xb_ref, wp_ref, bi_ref, taps_ref, pre_ref):
    nx, columns = inner_ref.shape[0], xa_ref.shape[1]
    h = bi_ref.shape[0]
    wp = wp_ref[...].astype(bf16)
    even_x = at_ref[0] % 2 == 0
    for x in range(2):
        a, b = row_of(xa_ref, x, 0, columns), row_of(xb_ref, x, 0, columns)
        taps_ref[x] = taps_along_z(lax.select(even_x, b, a))
        taps_ref[x + 2] = taps_along_z(lax.select(even_x, a, b))
    rows = [taps_ref[0], taps_ref[1], inner_ref[0], inner_ref[1], inner_ref[nx - 2], inner_ref[nx - 1], taps_ref[2], taps_ref[3]]
    for i, at in enumerate((0, 1, 4, 5)):
        patch = jnp.concatenate(rows[at : at + 3], axis=0)
        pre_ref[i] = window(dot(wp, stacked(patch)), h, (columns - 2) * 128, False) + bi_ref[...]


def coarse_kernel(factor, size_x, size_y, at_ref, inner_ref, outer_ref, pre_in_ref, pre_out_ref, vd_ref, ya_ref, yb_ref, xa_ref, xb_ref,
                  proj_ref, out_ref, q_ref, gpre_ref, low_ref, grads_ref,
                  act_s, g_s, sums, rests, g_sum):
    nx, ny, k = vd_ref.shape[0], vd_ref.shape[1], vd_ref.shape[2] // 2
    wide, own = (ny + 2) * 128, slice(128, 128 * (ny + 1))
    pj, pt = projections(proj_ref)
    bo = column(out_ref[...])
    even_x, even_y = at_ref[0] % 2 == 0, at_ref[1] % 2 == 0
    taps = [(outer_ref, 0), (outer_ref, 1)] + [(inner_ref, x) for x in range(nx)] + [(outer_ref, 2), (outer_ref, 3)]
    pres = [(pre_out_ref, 0), (pre_out_ref, 1)] + [(pre_in_ref, x) for x in range(nx - 2)] + [(pre_out_ref, 2), (pre_out_ref, 3)]
    low_x = jnp.where(at_ref[0] == 0, 0.0, 1.0)
    high_x = jnp.where(at_ref[0] == size_x - 1, 0.0, 1.0)
    low_y = jnp.where(at_ref[1] == 0, 0.0, 1.0)
    high_y = jnp.where(at_ref[1] == size_y - 1, 0.0, 1.0)

    def forward(x, vd, inside):
        pre_ref, at = pres[x]
        act, g, gpre, lower, lower_cot = coupling(pre_ref[at], vd[:k], vd[k:], pj, pt, bo)
        taps_ref, at = taps[x + 1]
        u = taps_ref[at][k : 2 * k, 128 : 128 + wide]
        for y in range(ny + 2):
            cols = slice(128 * y, 128 * (y + 1))
            here = inside * (low_y if y == 0 else high_y if y == ny + 1 else 1.0)
            q_ref[x, y, :k] = u[:, cols]
            q_ref[x, y, k:] = lower[:, cols] * here
        gpre_ref[x] = gpre
        return act, g, lower_cot

    sums[...] = jnp.zeros_like(sums)
    rests[...] = jnp.zeros_like(rests)
    g_sum[...] = jnp.zeros_like(g_sum)

    for x in range(nx):
        a, b = ya_ref[x, 0], yb_ref[x, 0]
        vd = jnp.concatenate([lax.select(even_y, b, a), row_of(vd_ref, x, 0, ny), lax.select(even_y, a, b)], axis=1)
        act, g, lower_cot = forward(x + 1, vd, 1.0)
        low_ref[x] = lower_cot[:, own]
        act_s[x] = act[:, own]
        g_s[x] = g[:, own]
    a, b = row_of(xa_ref, 0, 0, ny + 2), row_of(xb_ref, 0, 0, ny + 2)
    forward(0, lax.select(even_x, b, a), low_x)
    forward(nx + 1, lax.select(even_x, a, b), high_x)

    for x in range(nx):
        patch = jnp.concatenate([ref[at][:, 128 : 128 + wide] for ref, at in taps[x + 1 : x + 4]], axis=0)
        a, b = weight_products(patch, gpre_ref[x + 1][:, own], act_s[x], g_s[x])
        sums[...] += a
        rests[...] += b
        g_sum[...] += lane_sum(g_s[x])
    rows, fold = 9 * k, 9 * k // 2
    conv, bias_in, proj, bias_out = gathered(sums[...], rests[...], g_sum[...], rows, 2 * k, 64)
    grads_ref[:rows] = conv[:, :128] * factor
    second = conv[:, 128:] * factor
    grads_ref[rows : rows + fold] = lanes_from(64, pltpu.roll(second[fold:], 64, 1), second[:fold])
    proj = proj[:, 128:] * factor
    at = rows + fold
    grads_ref[at : at + k] = lanes_from(64, proj[k:], pltpu.roll(proj[:k], 64, 1))
    grads_ref[at + k : at + k + 8] = lanes_from(64, bias_out, bias_in[:, :128]) * factor
    grads_ref[at + k + 8 :] = jnp.zeros((grads_ref.shape[0] - at - k - 8, 128), f32)


def coarse_back_kernel(gpre_ref, low_ref, cot_ref, conv_ref, dq_ref):
    nx, ny, k = low_ref.shape[0], cot_ref.shape[1], low_ref.shape[1]
    wd = back_weight(conv_ref)

    def back(x, _):
        parts = jnp.concatenate([gpre_ref[x + 2], gpre_ref[x + 1], gpre_ref[x]], axis=0)
        s = window(dot(wd, stacked(parts)), 3 * k, ny * 128, True)
        du = s[k : 2 * k] + shifted(s[:k], -1) + shifted(s[2 * k :], 1)
        low = low_ref[x]
        for y in range(ny):
            cols = slice(128 * y, 128 * (y + 1))
            dq_ref[x, y, :k] = cot_ref[x, y] + du[:, cols]
            dq_ref[x, y, k:] = low[:, cols]
        return 0

    lax.fori_loop(0, nx, back, 0, unroll=True)


def finer_rows(field):
    c = field.shape[0] // 4
    a, b, d, e = [field[i * c : (i + 1) * c] for i in range(4)]
    sum_u, sum_l, dif_u, dif_l = a + b, d + e, a - b, d - e
    rows = []
    for p, q in ((sum_u, sum_l), (dif_u, dif_l)):
        even, odd = 0.5 * (p + q), 0.5 * (p - q)
        cols = []
        for k in range(even.shape[1] // 128):
            cols += [even[:, 128 * k : 128 * (k + 1)], odd[:, 128 * k : 128 * (k + 1)]]
        rows.append(jnp.concatenate(cols, axis=1))
    return rows


def fine_kernel(factor, q_ref, dq_ref, conv_ref, in_ref, proj_ref, out_ref,
                field_ref, cot_ref, gpre_ref, grads_ref, taps, v_s, dz_s, sums, rests, g_sum):
    nx, ny = field_ref.shape[0], field_ref.shape[1]
    k = field_ref.shape[2] // 2
    h = conv_ref.shape[2]
    wp = forward_weight(conv_ref, 8)
    pj, pt = projections(proj_ref)
    bi, bo = column(in_ref[...]), column(out_ref[...])
    cy = ny // 2

    for x in range(q_ref.shape[0]):
        pair = finer_rows(row_of(q_ref, x, 0, cy + 2))
        for r in (2 * x, 2 * x + 1):
            if 1 <= r <= nx + 2:
                z = pair[r - 2 * x]
                taps[r - 1] = taps_along_z(z[:k, 128 : 128 * (ny + 3)])
                if 2 <= r < nx + 2:
                    v_s[r - 2] = z[k:, 256 : 128 * (ny + 2)]
    for x in range(nx // 2):
        dz_s[2 * x], dz_s[2 * x + 1] = finer_rows(row_of(dq_ref, x, 0, cy))

    sums[...] = jnp.zeros_like(sums)
    rests[...] = jnp.zeros_like(rests)
    g_sum[...] = jnp.zeros_like(g_sum)

    for x in range(nx):
        patch = jnp.concatenate([taps[x], taps[x + 1], taps[x + 2]], axis=0)
        pre = window(dot(wp, stacked(patch, 8)), h, ny * 128, False) + bi
        dz = dz_s[x]
        act, g, gpre, lower, lower_cot = coupling(pre, v_s[x], dz[k:], pj, pt, bo)
        a, b = weight_products(patch, gpre, act, g)
        sums[...] += a
        rests[...] += b
        g_sum[...] += lane_sum(g)
        field = jnp.concatenate([taps[x + 1][k : 2 * k, 128 : 128 * (ny + 1)], lower], axis=0)
        cot = jnp.concatenate([dz[:k], lower_cot], axis=0)
        for y in range(ny):
            cols = slice(128 * y, 128 * (y + 1))
            field_ref[x, y] = field[:, cols]
            cot_ref[x, y] = cot[:, cols]
            gpre_ref[x, y] = gpre[:, cols]

    conv, bias_in, proj, bias_out = gathered(sums[...], rests[...], g_sum[...], 9 * k, 2 * k, 3 * h)
    spare = jnp.zeros((9 * k - 2 * k - 16, 128), f32)
    others = jnp.concatenate([proj, pltpu.roll(bias_in, h, 1), bias_out, spare], axis=0)
    grads_ref[: 9 * k] = lanes_from(3 * h, others, conv) * factor
    grads_ref[9 * k :] = jnp.zeros((grads_ref.shape[0] - 9 * k, 128), f32)


def fine_back_kernel(gpre_ref, cot_ref, conv_ref, out_ref, columns_ref, rows_ref, gpre_s):
    nx, ny = cot_ref.shape[0], cot_ref.shape[1]
    k = cot_ref.shape[2] // 2
    h = gpre_ref.shape[2]
    wd = back_weight(conv_ref)
    for x in (0, 1, nx + 2, nx + 3):
        gpre_s[x] = jnp.zeros((h, ny * 128), f32)

    def fill(x, _):
        gpre_s[x + 2] = row_of(gpre_ref, x, 0, ny)
        return 0

    lax.fori_loop(0, nx, fill, 0, unroll=True)

    def contributions(x):
        parts = jnp.concatenate([gpre_s[x + 2], gpre_s[x + 1], gpre_s[x]], axis=0)
        o = dot(wd, stacked(parts))
        s = [placed_at(o[b * 3 * k : (b + 1) * 3 * k], b, 2 - b) for b in range(3)]
        s = s[0] + s[1] + s[2]
        du = s[k : 2 * k] + shifted(s[:k], -1) + shifted(s[2 * k :], 1)
        columns_ref[0, x] = du[:, :128]
        columns_ref[1, x] = du[:, 128 * (ny + 1) :]
        return du

    def inner(x, _):
        du = contributions(x + 1)
        for y in range(ny):
            out_ref[x, y, :k] = cot_ref[x, y, :k] + du[:, 128 * (y + 1) : 128 * (y + 2)]
            out_ref[x, y, k:] = cot_ref[x, y, k:]
        return 0

    def outer(i, _):
        du = contributions(i * (nx + 1))
        for y in range(ny):
            rows_ref[i, y] = du[:, 128 * (y + 1) : 128 * (y + 2)]
        return 0

    lax.fori_loop(0, nx, inner, 0, unroll=True)
    lax.fori_loop(0, 2, outer, 0, unroll=True)


def corners_kernel(rows_ref, low_ref, high_ref, out_ref):
    count = out_ref.shape[1]
    for i, x in ((0, 0), (1, low_ref.shape[0] - 1)):
        for y in range(count):
            more = [ref[x] for ref, at in ((low_ref, 0), (high_ref, count - 1)) if at == y]
            out_ref[i, y] = sum(more, rows_ref[i, y])


def rims_kernel(cot_ref, low_ref, high_ref, below_ref, above_ref, out_ref):
    nx, ny, k = cot_ref.shape[0], cot_ref.shape[1], low_ref.shape[1]
    for x in range(nx):
        cells = []
        for y in range(ny):
            du = cot_ref[x, y, :k]
            for ref, at in ((low_ref, y == 0), (high_ref, y == ny - 1)):
                if at:
                    du = du + ref[x + 1]
            for ref, at in ((below_ref, x == 0), (above_ref, x == nx - 1)):
                if at:
                    du = du + ref[y]
            cells.append(jnp.concatenate([du, cot_ref[x, y, k:]], axis=0))
        out_ref[:, x] = jnp.swapaxes(jnp.stack(cells, axis=0), 0, 1)


def unpack_kernel(at_ref, coarse_ref, coarse_other, fine_ref, fine_other,
                  f_conv, f_in, f_proj, f_out, c_conv, c_in, c_proj, c_out, coarse, fine):
    first = at_ref[1] % 2 == 0
    for whole, mine, other in ((coarse, coarse_ref, coarse_other), (fine, fine_ref, fine_other)):
        rows = mine.shape[0]
        a, b = mine[...], other[...]
        whole[:rows] = lax.select(first, a, b)
        whole[rows:] = lax.select(first, b, a)

    k, h = c_conv.shape[1], c_conv.shape[2]
    rows, fold = 9 * k, 9 * k // 2
    ahead = coarse[:rows]
    second = coarse[rows : rows + fold]
    taps = [ahead, pltpu.roll(ahead, 64, 1), jnp.concatenate([second, pltpu.roll(second, 64, 1)], axis=0)]
    for t in range(27):
        a, b, c = t // 9, t // 3 % 3, t % 3
        c_conv[t] = taps[b][(3 * a + c) * k : (3 * a + c + 1) * k, :h]
    at = rows + fold
    proj = coarse[at : at + k]
    c_proj[:k] = proj[:, :h]
    c_proj[k:] = pltpu.roll(proj, 64, 1)[:, :h]
    biases = coarse[at + k : at + k + 8]
    c_in[...] = biases[:1, :h]
    c_out[...] = pltpu.roll(biases, 64, 1)[:1, : 2 * k]

    k, h = f_conv.shape[1], f_conv.shape[2]
    whole = fine[: 9 * k]
    parts = [whole] + [pltpu.roll(whole, 128 - b * h, 1) for b in (1, 2, 3)]
    for t in range(27):
        a, b, c = t // 9, t // 3 % 3, t % 3
        f_conv[t] = parts[b][(3 * a + c) * k : (3 * a + c + 1) * k, :h]
    f_proj[...] = parts[3][: 2 * k, :h]
    f_in[...] = parts[3][2 * k : 2 * k + 1, :h]
    f_out[...] = parts[3][2 * k + 8 : 2 * k + 9, : 2 * k]


def call(kernel, outs, scratch, flops, *args, scalars=False):
    specs = [pl.BlockSpec(memory_space=pltpu.VMEM)] * len(args)
    if scalars:
        specs[0] = pl.BlockSpec(memory_space=pltpu.SMEM)
    return pl.pallas_call(
        kernel,
        in_specs=specs,
        out_shape=[jax.ShapeDtypeStruct(s, f32) for s in outs],
        scratch_shapes=[pltpu.VMEM(s, f32) for s in scratch],
        compiler_params=pltpu.CompilerParams(vmem_limit_bytes=VMEM_BYTES),
        cost_estimate=pl.CostEstimate(flops=flops, bytes_accessed=1_000_000, transcendentals=0),
    )(*args)


def swapped(axis, one, two):
    size = lax.axis_size(axis)
    inner = [(i, i ^ 1) for i in range(size)]
    outer = []
    for i in range(1, size - 1, 2):
        outer += [(i, i + 1), (i + 1, i)]
    two = lax.ppermute(two, axis, outer)
    one = lax.ppermute(one, axis, inner)
    return one, two


def halos(axis, low, high):
    even = lax.axis_index(axis) % 2 == 0
    one, two = swapped(axis, jnp.where(even, high, low), jnp.where(even, low, high))
    return jnp.where(even, two, one), jnp.where(even, one, two)


def partner(x, mask):
    sizes = [lax.axis_size("gx"), lax.axis_size("gy")]
    pairs = []
    for i in range(sizes[0] * sizes[1]):
        gx, gy = divmod(i, sizes[1])
        to = (gx ^ mask[0], gy ^ mask[1])
        if to[0] < sizes[0] and to[1] < sizes[1]:
            pairs.append((i, to[0] * sizes[1] + to[1]))
    return lax.ppermute(x, ("gx", "gy"), pairs)


CORE, X_NEAR, X_FAR, Y_NEAR, Y_FAR = (0, 1), (0, 2), (0, 6), (1, 0), (3, 0)
Z_ONE, Z_TWO, Z_FAR = (4, 0), (8, 0), (12, 8)


def second_half(step):
    gx, gy = lax.axis_index("gx"), lax.axis_index("gy")
    if step == CORE:
        return gy % 2 == 1
    if step == X_NEAR:
        return (gy // 2 + gy // 4) % 2 == 1
    return (gx + gx // 2) % 2 == 1


def half_sum(x, step):
    rows = x.shape[0] // 2
    upper = second_half(step)
    first, second = x[:rows], x[rows:]
    return jnp.where(upper, second, first) + partner(jnp.where(upper, first, second), step)


def in_order(mine, other, step):
    upper = second_half(step)
    return jnp.concatenate([jnp.where(upper, other, mine), jnp.where(upper, mine, other)], axis=0)


def tied(x, *others):
    return lax.optimization_barrier((x, *others))


def partners(x, first, second):
    both = (first[0] ^ second[0], first[1] ^ second[1])
    return partner(x, first), partner(x, second), partner(x, both)


def quarter_sum(x, first, second):
    rows = x.shape[0] // 4
    one, two = second_half(first), second_half(second)
    mine, other = (jnp.where(two, x[a:b], x[c:d]) for a, b, c, d in
                   ((2 * rows, 4 * rows, 0, 2 * rows), (0, 2 * rows, 2 * rows, 4 * rows)))
    both = (first[0] ^ second[0], first[1] ^ second[1])
    kept = jnp.where(one, mine[rows:], mine[:rows])
    a = partner(jnp.where(one, mine[:rows], mine[rows:]), first)
    b = partner(jnp.where(one, other[rows:], other[:rows]), second)
    c = partner(jnp.where(one, other[:rows], other[rows:]), both)
    return (kept + a) + (b + c)


def four_sum(coarse, fine, first, second, *later):
    both = jnp.concatenate([coarse, fine], axis=0)
    a, b, c = partners(both, first, second)
    a, *later = tied(a, *later)
    both = (both + a) + (b + c)
    return both[: coarse.shape[0]], both[coarse.shape[0] :], *later


def pair_sum(coarse, fine, step):
    both = jnp.concatenate([coarse, fine], axis=0)
    both = both + partner(both, step)
    return both[: coarse.shape[0]], both[coarse.shape[0] :]


def four_whole(coarse, fine, first, second):
    cut = coarse.shape[0]
    a, b, c = partners(jnp.concatenate([coarse, fine], axis=0), first, second)
    mine, other = in_order(coarse, a[:cut], first), in_order(b[:cut], c[:cut], first)
    return in_order(mine, other, second), (fine + a[cut:]) + (b[cut:] + c[cut:])


def local(
    coarse_out,
    coarse_cot,
    fine_conv,
    fine_bias_in,
    fine_proj,
    fine_bias_out,
    coarse_conv,
    coarse_bias_in,
    coarse_proj,
    coarse_bias_out,
):
    channels, nx, ny, nz = coarse_out.shape
    k = channels // 2
    h = coarse_conv.shape[1]
    fk, fh = fine_conv.shape[2], fine_conv.shape[1]
    size_x, size_y = lax.axis_size("gx"), lax.axis_size("gy")
    factor = float(4 * nx * ny * nz * size_x * size_y) ** -0.5
    at = jnp.stack([lax.axis_index("gx"), lax.axis_index("gy")]).astype(jnp.int32)
    c_conv, f_conv = jnp.transpose(coarse_conv, (0, 2, 1)), jnp.transpose(fine_conv, (0, 2, 1))

    u, one, two = call(
        ends_kernel, [(nx, ny, k, nz), (nx, 2, k, nz), (nx, 2, k, nz)], [], 500_000_000, at, coarse_out, scalars=True
    )
    u_y = swapped("gy", one, two)
    vd, cot_u, one, two = call(
        ends_vd_kernel,
        [(nx, ny, 2 * k, nz), (nx, ny, k, nz), (nx, 1, 2 * k, nz), (nx, 1, 2 * k, nz)],
        [],
        500_000_000,
        at,
        coarse_out,
        coarse_cot,
        scalars=True,
    )
    vd_y = swapped("gy", one, two)
    u_x = swapped("gx", *call(sides_kernel, [(2, ny + 4, k, nz)] * 2, [], 500_000_000, at, u, *u_y, scalars=True))
    inner, pre_in, wp, b_in = call(
        conv_inner_kernel,
        [(nx, 3 * k, (ny + 4) * nz), (nx - 2, h, (ny + 2) * nz), (3 * h, 27 * k), (h, 1)],
        [],
        2_500_000_000,
        at,
        u,
        *u_y,
        c_conv,
        coarse_bias_in[None, :],
        scalars=True,
    )
    vd_x = swapped("gx", *call(sides_kernel, [(1, ny + 2, 2 * k, nz)] * 2, [], 500_000_000, at, vd, *vd_y, scalars=True))
    outer, pre_out = call(
        conv_outer_kernel,
        [(4, 3 * k, (ny + 4) * nz), (4, h, (ny + 2) * nz)],
        [],
        4_000_000_000,
        at,
        inner,
        *u_x,
        wp,
        b_in,
        scalars=True,
    )
    q, c_gpre, low, coarse_grads = call(
        lambda *refs: coarse_kernel(factor, size_x, size_y, *refs),
        [(nx + 2, ny + 2, 2 * k, nz), (nx + 2, h, (ny + 2) * nz), (nx, k, ny * nz), (16 * k, 128)],
        [
            (nx, h, ny * nz),
            (nx, 2 * k, ny * nz),
            (9 * k + 16 + 2 * k, 4 * h),
            (9 * k + 2 * k, 4 * h),
            (2 * k, 128),
        ],
        6_000_000_000,
        at,
        inner,
        outer,
        pre_in,
        pre_out,
        vd,
        *vd_y,
        *vd_x,
        coarse_proj,
        coarse_bias_out[None, :],
        scalars=True,
    )
    coarse_grads = half_sum(coarse_grads, CORE)
    (dq,) = call(coarse_back_kernel, [(nx, ny, 2 * k, nz)], [], 2_500_000_000, c_gpre, low, cot_u, c_conv)
    coarse_grads, q, dq = tied(coarse_grads, q, dq)
    coarse_grads = quarter_sum(coarse_grads, X_NEAR, Y_NEAR)

    fx, fy = 2 * nx, 2 * ny
    field, cot, gpre, fine_grads = call(
        lambda *refs: fine_kernel(factor, *refs),
        [(fx, fy, 2 * fk, nz), (fx, fy, 2 * fk, nz), (fx, fy, fh, nz), (10 * fk, 128)],
        [
            (fx + 2, 3 * fk, (fy + 2) * nz),
            (fx, fk, fy * nz),
            (fx, 2 * fk, fy * nz),
            (9 * fk + 16 + 2 * fk, 4 * fh),
            (9 * fk + 2 * fk, 4 * fh),
            (2 * fk, 128),
        ],
        9_000_000_000,
        q,
        dq,
        f_conv,
        fine_bias_in[None, :],
        fine_proj,
        fine_bias_out[None, :],
    )
    coarse_grads, fine_grads = tied(coarse_grads, fine_grads)
    fine_grads = half_sum(fine_grads, CORE)

    sums = four_sum(coarse_grads, fine_grads, X_FAR, Y_FAR)
    *sums, gpre = four_sum(*sums, Z_ONE, Z_TWO, gpre)
    cot, columns, rows = call(
        fine_back_kernel,
        [cot.shape, (2, fx + 2, fk, nz), (2, fy, fk, nz)],
        [(fx + 4, fh, fy * nz)],
        4_000_000_000,
        gpre,
        cot,
        f_conv,
    )
    low, high = halos("gy", columns[0], columns[1])
    (rows,) = call(corners_kernel, [rows.shape], [], 6_000_000_000, rows, low, high)
    below, above = halos("gx", rows[0], rows[1])
    sums = pair_sum(*sums, Z_FAR)
    (cot,) = call(rims_kernel, [(2 * fk, fx, fy, nz)], [], 2_000_000_000, cot, low, high, below, above)
    coarse_grads, fine_grads = four_whole(*sums, X_NEAR, Y_NEAR)
    other = partner(jnp.concatenate([coarse_grads, fine_grads], axis=0), CORE)
    cut = coarse_grads.shape[0]
    sums = (coarse_grads, other[:cut], fine_grads, other[cut:])

    grads = call(
        unpack_kernel,
        [(27, fk, fh), (1, fh), (2 * fk, fh), (1, 2 * fk), (27, k, h), (1, h), (2 * k, h), (1, 2 * k)],
        [(16 * k, 128), (10 * fk, 128)],
        1_000_000,
        at,
        *sums,
        scalars=True,
    )
    f_conv, f_in, f_proj, f_out, c_conv, c_in, c_proj, c_out = grads
    return (
        jnp.transpose(field, (2, 0, 1, 3)),
        cot,
        jnp.transpose(f_conv, (0, 2, 1)),
        f_in[0],
        f_proj,
        f_out[0],
        jnp.transpose(c_conv, (0, 2, 1)),
        c_in[0],
        c_proj,
        c_out[0],
    )


def solution(mesh):
    split_field = P(None, "gx", "gy", None)
    return jax.shard_map(
        local,
        mesh=mesh,
        in_specs=(split_field, split_field) + (P(),) * 8,
        out_specs=(split_field, split_field) + (P(),) * 8,
        check_vma=False,
    )
```

```python
import jax
import jax.numpy as jnp
from jax import lax
from jax.experimental import pallas as pl
from jax.experimental.pallas import tpu as pltpu
from jax.sharding import PartitionSpec as P

f32 = jnp.float32
bf16 = jnp.bfloat16
VMEM_BYTES = 24 * 1024 * 1024


def dot(a, b):
    return lax.dot_general(a, b, (((1,), (0,)), ((), ())), preferred_element_type=f32)


def dot_cells(a, b):
    return lax.dot_general(a, b, (((1,), (1,)), ((), ())), preferred_element_type=f32)


def split(x):
    top = x.astype(bf16).astype(f32)
    return top, x - top


def stacked(x, spare=0):
    top, rest = split(x)
    rows = [top, rest, top]
    if spare:
        rows.append(jnp.zeros((spare, x.shape[1]), f32))
    return jnp.concatenate(rows, axis=0).astype(bf16)


def thrice(x):
    top, rest = split(x)
    return jnp.concatenate([top, top, rest], axis=0)


def row_of(ref, x, first, count):
    return jnp.concatenate([ref[x, first + y] for y in range(count)], axis=1)


def shifted(x, step):
    lane = lax.broadcasted_iota(jnp.int32, (x.shape[0], 128), 1)
    edge = 0 if step > 0 else 127
    out = []
    for k in range(x.shape[1] // 128):
        moved = pltpu.roll(x[:, 128 * k : 128 * (k + 1)], step % 128, 1)
        out.append(jnp.where(lane == edge, 0.0, moved))
    return jnp.concatenate(out, axis=1)


def taps_along_z(x):
    return jnp.concatenate([shifted(x, 1), x, shifted(x, -1)], axis=0)


def window(o, rows, width, backward):
    parts = []
    for b in range(3):
        at = (2 - b if backward else b) * 128
        parts.append(o[b * rows : (b + 1) * rows, at : at + width])
    return parts[0] + parts[1] + parts[2]


def coupling(pre, v, dv, pj, pt, bo):
    half = v.shape[0]
    sig = jax.nn.sigmoid(pre)
    act = pre * sig
    out = dot(pj, stacked(act)) + bo
    sc = jnp.tanh(out[:half])
    centred = v - out[half:]
    lower = centred * jnp.exp(-sc)
    lower_cot = dv * jnp.exp(sc)
    g = jnp.concatenate([dv * centred * (1.0 - sc * sc), dv], axis=0)
    ga = dot(pt, stacked(g))
    gpre = ga * sig * (1.0 + pre * (1.0 - sig))
    return act, g, gpre, lower, lower_cot


def placed_at(x, before, after):
    rows = x.shape[0]
    parts = []
    if before:
        parts.append(jnp.zeros((rows, 128 * before), f32))
    parts.append(x)
    if after:
        parts.append(jnp.zeros((rows, 128 * after), f32))
    return jnp.concatenate(parts, axis=1) if len(parts) > 1 else x


def weight_products(patch, gpre, act, g):
    tops, rests = [], []
    for piece in [placed_at(gpre, b, 2 - b) for b in range(3)] + [placed_at(act, 1, 1)]:
        top, rest = split(piece)
        tops.append(top)
        rests.append(rest)
    right = jnp.concatenate(tops + rests, axis=0).astype(bf16)
    p_top, p_rest = split(patch)
    g_top, g_rest = split(placed_at(g, 1, 1))
    ones = jnp.ones((16, patch.shape[1]), f32)
    first = jnp.concatenate([p_top, ones, g_top], axis=0).astype(bf16)
    second = jnp.concatenate([p_rest, g_rest], axis=0).astype(bf16)
    wide = right.shape[0] // 2
    if wide < 256:
        both = dot_cells(jnp.concatenate([first, second], axis=0), right)
        a, b = both[: first.shape[0]], both[first.shape[0] :, :wide]
    else:
        a, b = dot_cells(first, right), dot_cells(second, right[:wide])
    return a[:, :wide] + a[:, wide:], b


def lane_sum(x):
    total = x[:, :128]
    for k in range(1, x.shape[1] // 128):
        total = total + x[:, 128 * k : 128 * (k + 1)]
    return total


def gathered(first, second, g_sum, taps, outs, lane_of_outs):
    conv = first[:taps] + second[:taps]
    bias_in = first[taps : taps + 8]
    proj = first[taps + 16 :] + second[taps:]
    total = jnp.broadcast_to(jnp.sum(g_sum, axis=1, keepdims=True), (outs, 128))
    row = lax.broadcasted_iota(jnp.int32, (outs, 128), 0)
    lane = lax.broadcasted_iota(jnp.int32, (outs, 128), 1)
    bias_out = jnp.sum(jnp.where(lane == row + lane_of_outs, total, 0.0), axis=0, keepdims=True)
    return conv, bias_in, proj, jnp.broadcast_to(bias_out, (8, 128))


def lanes_from(at, upper, lower):
    lane = lax.broadcasted_iota(jnp.int32, upper.shape, 1)
    return jnp.where(lane >= at, upper, lower)


def column(row):
    n = row.shape[1]
    i = lax.broadcasted_iota(jnp.int32, (n, n), 0)
    j = lax.broadcasted_iota(jnp.int32, (n, n), 1)
    return jnp.sum(jnp.where(i == j, jnp.broadcast_to(row, (n, n)), 0.0), axis=1, keepdims=True)


def forward_weight(conv_ref, spare):
    h = conv_ref.shape[2]
    parts = []
    for b in range(3):
        w = jnp.concatenate([conv_ref[9 * a + 3 * b + c] for a in range(3) for c in range(3)], axis=0)
        rows = thrice(w)
        if spare:
            rows = jnp.concatenate([rows, jnp.zeros((spare, h), f32)], axis=0)
        parts.append(rows.T)
    return jnp.concatenate(parts, axis=0).astype(bf16)


def back_weight(conv_ref):
    w = [jnp.concatenate([conv_ref[9 * a + t] for t in range(9)], axis=0).T for a in range(3)]
    return thrice(jnp.concatenate(w, axis=0)).T.astype(bf16)


def projections(proj_ref):
    p = proj_ref[...]
    return thrice(p.T).T.astype(bf16), thrice(p).T.astype(bf16)


def transposed_block(ref, first, last, x):
    return jnp.swapaxes(ref[first:last, x], 0, 1)


def ends_kernel(at_ref, w_ref, u_ref, one_ref, two_ref):
    nx, ny, k = u_ref.shape[0], u_ref.shape[1], u_ref.shape[2]
    even = at_ref[1] % 2 == 0
    for x in range(nx):
        u = transposed_block(w_ref, 0, k, x)
        u_ref[x] = u
        low, high = u[:2], u[ny - 2 :]
        one_ref[x] = lax.select(even, high, low)
        two_ref[x] = lax.select(even, low, high)


def ends_vd_kernel(at_ref, w_ref, dw_ref, vd_ref, cot_ref, one_ref, two_ref):
    nx, ny, k = cot_ref.shape[0], cot_ref.shape[1], cot_ref.shape[2]
    even = at_ref[1] % 2 == 0
    for x in range(nx):
        cot_ref[x] = transposed_block(dw_ref, 0, k, x)
        vd = jnp.concatenate([transposed_block(w_ref, k, 2 * k, x), transposed_block(dw_ref, k, 2 * k, x)], axis=1)
        vd_ref[x] = vd
        low, high = vd[:1], vd[ny - 1 :]
        one_ref[x] = lax.select(even, high, low)
        two_ref[x] = lax.select(even, low, high)


def sides_kernel(at_ref, f_ref, ya_ref, yb_ref, one_ref, two_ref):
    nx, rows = f_ref.shape[0], one_ref.shape[0]
    even_x, even_y = at_ref[0] % 2 == 0, at_ref[1] % 2 == 0

    def widened(x):
        a, b = ya_ref[x], yb_ref[x]
        return jnp.concatenate([lax.select(even_y, b, a), f_ref[x], lax.select(even_y, a, b)], axis=0)

    for x in range(rows):
        low, high = widened(x), widened(nx - rows + x)
        one_ref[x] = lax.select(even_x, high, low)
        two_ref[x] = lax.select(even_x, low, high)


def conv_inner_kernel(at_ref, u_ref, ya_ref, yb_ref, conv_ref, in_ref, taps_ref, pre_ref, wp_ref, bi_ref):
    nx, ny, k = u_ref.shape[0], u_ref.shape[1], u_ref.shape[2]
    h = conv_ref.shape[2]
    wp = forward_weight(conv_ref, 0)
    wp_ref[...] = wp.astype(f32)
    bi = column(in_ref[...])
    bi_ref[...] = bi
    even_y = at_ref[1] % 2 == 0
    taps = []
    for x in range(nx):
        a, b = row_of(ya_ref, x, 0, 2), row_of(yb_ref, x, 0, 2)
        low, high = lax.select(even_y, b, a), lax.select(even_y, a, b)
        taps_ref[x] = taps_along_z(jnp.concatenate([low, row_of(u_ref, x, 0, ny), high], axis=1))
    for x in range(nx - 2):
        patch = jnp.concatenate([taps_ref[x], taps_ref[x + 1], taps_ref[x + 2]], axis=0)
        pre_ref[x] = window(dot(wp, stacked(patch)), h, (ny + 2) * 128, False) + bi


def conv_outer_kernel(at_ref, inner_ref, xa_ref, xb_ref, wp_ref, bi_ref, taps_ref, pre_ref):
    nx, columns = inner_ref.shape[0], xa_ref.shape[1]
    h = bi_ref.shape[0]
    wp = wp_ref[...].astype(bf16)
    even_x = at_ref[0] % 2 == 0
    for x in range(2):
        a, b = row_of(xa_ref, x, 0, columns), row_of(xb_ref, x, 0, columns)
        taps_ref[x] = taps_along_z(lax.select(even_x, b, a))
        taps_ref[x + 2] = taps_along_z(lax.select(even_x, a, b))
    rows = [taps_ref[0], taps_ref[1], inner_ref[0], inner_ref[1], inner_ref[nx - 2], inner_ref[nx - 1], taps_ref[2], taps_ref[3]]
    for i, at in enumerate((0, 1, 4, 5)):
        patch = jnp.concatenate(rows[at : at + 3], axis=0)
        pre_ref[i] = window(dot(wp, stacked(patch)), h, (columns - 2) * 128, False) + bi_ref[...]


def coarse_kernel(factor, size_x, size_y, at_ref, inner_ref, outer_ref, pre_in_ref, pre_out_ref, vd_ref, ya_ref, yb_ref, xa_ref, xb_ref,
                  proj_ref, out_ref, q_ref, gpre_ref, low_ref, grads_ref,
                  act_s, g_s, sums, rests, g_sum):
    nx, ny, k = vd_ref.shape[0], vd_ref.shape[1], vd_ref.shape[2] // 2
    wide, own = (ny + 2) * 128, slice(128, 128 * (ny + 1))
    pj, pt = projections(proj_ref)
    bo = column(out_ref[...])
    even_x, even_y = at_ref[0] % 2 == 0, at_ref[1] % 2 == 0
    taps = [(outer_ref, 0), (outer_ref, 1)] + [(inner_ref, x) for x in range(nx)] + [(outer_ref, 2), (outer_ref, 3)]
    pres = [(pre_out_ref, 0), (pre_out_ref, 1)] + [(pre_in_ref, x) for x in range(nx - 2)] + [(pre_out_ref, 2), (pre_out_ref, 3)]
    low_x = jnp.where(at_ref[0] == 0, 0.0, 1.0)
    high_x = jnp.where(at_ref[0] == size_x - 1, 0.0, 1.0)
    low_y = jnp.where(at_ref[1] == 0, 0.0, 1.0)
    high_y = jnp.where(at_ref[1] == size_y - 1, 0.0, 1.0)

    def forward(x, vd, inside):
        pre_ref, at = pres[x]
        act, g, gpre, lower, lower_cot = coupling(pre_ref[at], vd[:k], vd[k:], pj, pt, bo)
        taps_ref, at = taps[x + 1]
        u = taps_ref[at][k : 2 * k, 128 : 128 + wide]
        for y in range(ny + 2):
            cols = slice(128 * y, 128 * (y + 1))
            here = inside * (low_y if y == 0 else high_y if y == ny + 1 else 1.0)
            q_ref[x, y, :k] = u[:, cols]
            q_ref[x, y, k:] = lower[:, cols] * here
        gpre_ref[x] = gpre
        return act, g, lower_cot

    sums[...] = jnp.zeros_like(sums)
    rests[...] = jnp.zeros_like(rests)
    g_sum[...] = jnp.zeros_like(g_sum)

    for x in range(nx):
        a, b = ya_ref[x, 0], yb_ref[x, 0]
        vd = jnp.concatenate([lax.select(even_y, b, a), row_of(vd_ref, x, 0, ny), lax.select(even_y, a, b)], axis=1)
        act, g, lower_cot = forward(x + 1, vd, 1.0)
        low_ref[x] = lower_cot[:, own]
        act_s[x] = act[:, own]
        g_s[x] = g[:, own]
    a, b = row_of(xa_ref, 0, 0, ny + 2), row_of(xb_ref, 0, 0, ny + 2)
    forward(0, lax.select(even_x, b, a), low_x)
    forward(nx + 1, lax.select(even_x, a, b), high_x)

    for x in range(nx):
        patch = jnp.concatenate([ref[at][:, 128 : 128 + wide] for ref, at in taps[x + 1 : x + 4]], axis=0)
        a, b = weight_products(patch, gpre_ref[x + 1][:, own], act_s[x], g_s[x])
        sums[...] += a
        rests[...] += b
        g_sum[...] += lane_sum(g_s[x])
    rows, fold = 9 * k, 9 * k // 2
    conv, bias_in, proj, bias_out = gathered(sums[...], rests[...], g_sum[...], rows, 2 * k, 64)
    grads_ref[:rows] = conv[:, :128] * factor
    second = conv[:, 128:] * factor
    grads_ref[rows : rows + fold] = lanes_from(64, pltpu.roll(second[fold:], 64, 1), second[:fold])
    proj = proj[:, 128:] * factor
    at = rows + fold
    grads_ref[at : at + k] = lanes_from(64, proj[k:], pltpu.roll(proj[:k], 64, 1))
    grads_ref[at + k : at + k + 8] = lanes_from(64, bias_out, bias_in[:, :128]) * factor
    grads_ref[at + k + 8 :] = jnp.zeros((grads_ref.shape[0] - at - k - 8, 128), f32)


def coarse_back_kernel(gpre_ref, low_ref, cot_ref, conv_ref, dq_ref):
    nx, ny, k = low_ref.shape[0], cot_ref.shape[1], low_ref.shape[1]
    wd = back_weight(conv_ref)

    def back(x, _):
        parts = jnp.concatenate([gpre_ref[x + 2], gpre_ref[x + 1], gpre_ref[x]], axis=0)
        s = window(dot(wd, stacked(parts)), 3 * k, ny * 128, True)
        du = s[k : 2 * k] + shifted(s[:k], -1) + shifted(s[2 * k :], 1)
        low = low_ref[x]
        for y in range(ny):
            cols = slice(128 * y, 128 * (y + 1))
            dq_ref[x, y, :k] = cot_ref[x, y] + du[:, cols]
            dq_ref[x, y, k:] = low[:, cols]
        return 0

    lax.fori_loop(0, nx, back, 0, unroll=True)


def finer_rows(field):
    c = field.shape[0] // 4
    a, b, d, e = [field[i * c : (i + 1) * c] for i in range(4)]
    sum_u, sum_l, dif_u, dif_l = a + b, d + e, a - b, d - e
    rows = []
    for p, q in ((sum_u, sum_l), (dif_u, dif_l)):
        even, odd = 0.5 * (p + q), 0.5 * (p - q)
        cols = []
        for k in range(even.shape[1] // 128):
            cols += [even[:, 128 * k : 128 * (k + 1)], odd[:, 128 * k : 128 * (k + 1)]]
        rows.append(jnp.concatenate(cols, axis=1))
    return rows


def fine_kernel(factor, q_ref, dq_ref, conv_ref, in_ref, proj_ref, out_ref,
                field_ref, cot_ref, gpre_ref, grads_ref, taps, v_s, dz_s, sums, rests, g_sum):
    nx, ny = field_ref.shape[0], field_ref.shape[1]
    k = field_ref.shape[2] // 2
    h = conv_ref.shape[2]
    wp = forward_weight(conv_ref, 8)
    pj, pt = projections(proj_ref)
    bi, bo = column(in_ref[...]), column(out_ref[...])
    cy = ny // 2

    for x in range(q_ref.shape[0]):
        pair = finer_rows(row_of(q_ref, x, 0, cy + 2))
        for r in (2 * x, 2 * x + 1):
            if 1 <= r <= nx + 2:
                z = pair[r - 2 * x]
                taps[r - 1] = taps_along_z(z[:k, 128 : 128 * (ny + 3)])
                if 2 <= r < nx + 2:
                    v_s[r - 2] = z[k:, 256 : 128 * (ny + 2)]
    for x in range(nx // 2):
        dz_s[2 * x], dz_s[2 * x + 1] = finer_rows(row_of(dq_ref, x, 0, cy))

    sums[...] = jnp.zeros_like(sums)
    rests[...] = jnp.zeros_like(rests)
    g_sum[...] = jnp.zeros_like(g_sum)

    for x in range(nx):
        patch = jnp.concatenate([taps[x], taps[x + 1], taps[x + 2]], axis=0)
        pre = window(dot(wp, stacked(patch, 8)), h, ny * 128, False) + bi
        dz = dz_s[x]
        act, g, gpre, lower, lower_cot = coupling(pre, v_s[x], dz[k:], pj, pt, bo)
        a, b = weight_products(patch, gpre, act, g)
        sums[...] += a
        rests[...] += b
        g_sum[...] += lane_sum(g)
        field = jnp.concatenate([taps[x + 1][k : 2 * k, 128 : 128 * (ny + 1)], lower], axis=0)
        cot = jnp.concatenate([dz[:k], lower_cot], axis=0)
        for y in range(ny):
            cols = slice(128 * y, 128 * (y + 1))
            field_ref[x, y] = field[:, cols]
            cot_ref[x, y] = cot[:, cols]
            gpre_ref[x, y] = gpre[:, cols]

    conv, bias_in, proj, bias_out = gathered(sums[...], rests[...], g_sum[...], 9 * k, 2 * k, 3 * h)
    spare = jnp.zeros((9 * k - 2 * k - 16, 128), f32)
    others = jnp.concatenate([proj, pltpu.roll(bias_in, h, 1), bias_out, spare], axis=0)
    grads_ref[: 9 * k] = lanes_from(3 * h, others, conv) * factor
    grads_ref[9 * k :] = jnp.zeros((grads_ref.shape[0] - 9 * k, 128), f32)


def fine_back_kernel(gpre_ref, cot_ref, conv_ref, out_ref, columns_ref, rows_ref, gpre_s):
    nx, ny = cot_ref.shape[0], cot_ref.shape[1]
    k = cot_ref.shape[2] // 2
    h = gpre_ref.shape[2]
    wd = back_weight(conv_ref)
    for x in (0, 1, nx + 2, nx + 3):
        gpre_s[x] = jnp.zeros((h, ny * 128), f32)

    def fill(x, _):
        gpre_s[x + 2] = row_of(gpre_ref, x, 0, ny)
        return 0

    lax.fori_loop(0, nx, fill, 0, unroll=True)

    def contributions(x):
        parts = jnp.concatenate([gpre_s[x + 2], gpre_s[x + 1], gpre_s[x]], axis=0)
        o = dot(wd, stacked(parts))
        s = [placed_at(o[b * 3 * k : (b + 1) * 3 * k], b, 2 - b) for b in range(3)]
        s = s[0] + s[1] + s[2]
        du = s[k : 2 * k] + shifted(s[:k], -1) + shifted(s[2 * k :], 1)
        columns_ref[0, x] = du[:, :128]
        columns_ref[1, x] = du[:, 128 * (ny + 1) :]
        return du

    def inner(x, _):
        du = contributions(x + 1)
        for y in range(ny):
            out_ref[x, y, :k] = cot_ref[x, y, :k] + du[:, 128 * (y + 1) : 128 * (y + 2)]
            out_ref[x, y, k:] = cot_ref[x, y, k:]
        return 0

    def outer(i, _):
        du = contributions(i * (nx + 1))
        for y in range(ny):
            rows_ref[i, y] = du[:, 128 * (y + 1) : 128 * (y + 2)]
        return 0

    lax.fori_loop(0, nx, inner, 0, unroll=True)
    lax.fori_loop(0, 2, outer, 0, unroll=True)


def corners_kernel(rows_ref, low_ref, high_ref, out_ref):
    count = out_ref.shape[1]
    for i, x in ((0, 0), (1, low_ref.shape[0] - 1)):
        for y in range(count):
            more = [ref[x] for ref, at in ((low_ref, 0), (high_ref, count - 1)) if at == y]
            out_ref[i, y] = sum(more, rows_ref[i, y])


def channels_first_kernel(field_ref, out_ref):
    for x in range(field_ref.shape[0]):
        out_ref[:, x] = jnp.swapaxes(field_ref[x], 0, 1)


def rims_kernel(cot_ref, low_ref, high_ref, below_ref, above_ref, out_ref):
    nx, ny, k = cot_ref.shape[0], cot_ref.shape[1], low_ref.shape[1]
    for x in range(nx):
        cells = []
        for y in range(ny):
            du = cot_ref[x, y, :k]
            for ref, at in ((low_ref, y == 0), (high_ref, y == ny - 1)):
                if at:
                    du = du + ref[x + 1]
            for ref, at in ((below_ref, x == 0), (above_ref, x == nx - 1)):
                if at:
                    du = du + ref[y]
            cells.append(jnp.concatenate([du, cot_ref[x, y, k:]], axis=0))
        out_ref[:, x] = jnp.swapaxes(jnp.stack(cells, axis=0), 0, 1)


def unpack_kernel(at_ref, coarse_ref, coarse_other, fine_ref, fine_other,
                  f_conv, f_in, f_proj, f_out, c_conv, c_in, c_proj, c_out, coarse, fine):
    first = at_ref[1] % 2 == 0
    for whole, mine, other in ((coarse, coarse_ref, coarse_other), (fine, fine_ref, fine_other)):
        rows = mine.shape[0]
        a, b = mine[...], other[...]
        whole[:rows] = lax.select(first, a, b)
        whole[rows:] = lax.select(first, b, a)

    k, h = c_conv.shape[1], c_conv.shape[2]
    rows, fold = 9 * k, 9 * k // 2
    ahead = coarse[:rows]
    second = coarse[rows : rows + fold]
    taps = [ahead, pltpu.roll(ahead, 64, 1), jnp.concatenate([second, pltpu.roll(second, 64, 1)], axis=0)]
    for t in range(27):
        a, b, c = t // 9, t // 3 % 3, t % 3
        c_conv[t] = taps[b][(3 * a + c) * k : (3 * a + c + 1) * k, :h]
    at = rows + fold
    proj = coarse[at : at + k]
    c_proj[:k] = proj[:, :h]
    c_proj[k:] = pltpu.roll(proj, 64, 1)[:, :h]
    biases = coarse[at + k : at + k + 8]
    c_in[...] = biases[:1, :h]
    c_out[...] = pltpu.roll(biases, 64, 1)[:1, : 2 * k]

    k, h = f_conv.shape[1], f_conv.shape[2]
    whole = fine[: 9 * k]
    parts = [whole] + [pltpu.roll(whole, 128 - b * h, 1) for b in (1, 2, 3)]
    for t in range(27):
        a, b, c = t // 9, t // 3 % 3, t % 3
        f_conv[t] = parts[b][(3 * a + c) * k : (3 * a + c + 1) * k, :h]
    f_proj[...] = parts[3][: 2 * k, :h]
    f_in[...] = parts[3][2 * k : 2 * k + 1, :h]
    f_out[...] = parts[3][2 * k + 8 : 2 * k + 9, : 2 * k]


def call(kernel, outs, scratch, flops, *args, scalars=False):
    specs = [pl.BlockSpec(memory_space=pltpu.VMEM)] * len(args)
    if scalars:
        specs[0] = pl.BlockSpec(memory_space=pltpu.SMEM)
    return pl.pallas_call(
        kernel,
        in_specs=specs,
        out_shape=[jax.ShapeDtypeStruct(s, f32) for s in outs],
        scratch_shapes=[pltpu.VMEM(s, f32) for s in scratch],
        compiler_params=pltpu.CompilerParams(vmem_limit_bytes=VMEM_BYTES),
        cost_estimate=pl.CostEstimate(flops=flops, bytes_accessed=1_000_000, transcendentals=0),
    )(*args)


def swapped(axis, one, two):
    size = lax.axis_size(axis)
    inner = [(i, i ^ 1) for i in range(size)]
    outer = []
    for i in range(1, size - 1, 2):
        outer += [(i, i + 1), (i + 1, i)]
    two = lax.ppermute(two, axis, outer)
    one = lax.ppermute(one, axis, inner)
    return one, two


def halos(axis, low, high):
    even = lax.axis_index(axis) % 2 == 0
    one, two = swapped(axis, jnp.where(even, high, low), jnp.where(even, low, high))
    return jnp.where(even, two, one), jnp.where(even, one, two)


def partner(x, mask):
    sizes = [lax.axis_size("gx"), lax.axis_size("gy")]
    pairs = []
    for i in range(sizes[0] * sizes[1]):
        gx, gy = divmod(i, sizes[1])
        to = (gx ^ mask[0], gy ^ mask[1])
        if to[0] < sizes[0] and to[1] < sizes[1]:
            pairs.append((i, to[0] * sizes[1] + to[1]))
    return lax.ppermute(x, ("gx", "gy"), pairs)


CORE, X_NEAR, X_FAR, Y_NEAR, Y_FAR = (0, 1), (0, 2), (0, 6), (1, 0), (3, 0)
Z_ONE, Z_TWO, Z_FAR = (4, 0), (8, 0), (12, 8)


def second_half(step):
    gx, gy = lax.axis_index("gx"), lax.axis_index("gy")
    if step == CORE:
        return gy % 2 == 1
    if step == X_NEAR:
        return (gy // 2 + gy // 4) % 2 == 1
    return (gx + gx // 2) % 2 == 1


def half_sum(x, step):
    rows = x.shape[0] // 2
    upper = second_half(step)
    first, second = x[:rows], x[rows:]
    return jnp.where(upper, second, first) + partner(jnp.where(upper, first, second), step)


def in_order(mine, other, step):
    upper = second_half(step)
    return jnp.concatenate([jnp.where(upper, other, mine), jnp.where(upper, mine, other)], axis=0)


def tied(x, *others):
    return lax.optimization_barrier((x, *others))


def partners(x, first, second):
    both = (first[0] ^ second[0], first[1] ^ second[1])
    return partner(x, first), partner(x, second), partner(x, both)


def quarter_sum(x, first, second):
    rows = x.shape[0] // 4
    one, two = second_half(first), second_half(second)
    mine, other = (jnp.where(two, x[a:b], x[c:d]) for a, b, c, d in
                   ((2 * rows, 4 * rows, 0, 2 * rows), (0, 2 * rows, 2 * rows, 4 * rows)))
    both = (first[0] ^ second[0], first[1] ^ second[1])
    kept = jnp.where(one, mine[rows:], mine[:rows])
    a = partner(jnp.where(one, mine[:rows], mine[rows:]), first)
    b = partner(jnp.where(one, other[rows:], other[:rows]), second)
    c = partner(jnp.where(one, other[:rows], other[rows:]), both)
    return (kept + a) + (b + c)


def four_sum(coarse, fine, first, second, *later):
    both = jnp.concatenate([coarse, fine], axis=0)
    a, b, c = partners(both, first, second)
    a, *later = tied(a, *later)
    both = (both + a) + (b + c)
    return both[: coarse.shape[0]], both[coarse.shape[0] :], *later


def pair_sum(coarse, fine, step):
    both = jnp.concatenate([coarse, fine], axis=0)
    both = both + partner(both, step)
    return both[: coarse.shape[0]], both[coarse.shape[0] :]


def four_whole(coarse, fine, first, second):
    cut = coarse.shape[0]
    a, b, c = partners(jnp.concatenate([coarse, fine], axis=0), first, second)
    mine, other = in_order(coarse, a[:cut], first), in_order(b[:cut], c[:cut], first)
    return in_order(mine, other, second), (fine + a[cut:]) + (b[cut:] + c[cut:])


def local(
    coarse_out,
    coarse_cot,
    fine_conv,
    fine_bias_in,
    fine_proj,
    fine_bias_out,
    coarse_conv,
    coarse_bias_in,
    coarse_proj,
    coarse_bias_out,
):
    channels, nx, ny, nz = coarse_out.shape
    k = channels // 2
    h = coarse_conv.shape[1]
    fk, fh = fine_conv.shape[2], fine_conv.shape[1]
    size_x, size_y = lax.axis_size("gx"), lax.axis_size("gy")
    factor = float(4 * nx * ny * nz * size_x * size_y) ** -0.5
    at = jnp.stack([lax.axis_index("gx"), lax.axis_index("gy")]).astype(jnp.int32)
    c_conv, f_conv = jnp.transpose(coarse_conv, (0, 2, 1)), jnp.transpose(fine_conv, (0, 2, 1))

    u, one, two = call(
        ends_kernel, [(nx, ny, k, nz), (nx, 2, k, nz), (nx, 2, k, nz)], [], 500_000_000, at, coarse_out, scalars=True
    )
    u_y = swapped("gy", one, two)
    vd, cot_u, one, two = call(
        ends_vd_kernel,
        [(nx, ny, 2 * k, nz), (nx, ny, k, nz), (nx, 1, 2 * k, nz), (nx, 1, 2 * k, nz)],
        [],
        500_000_000,
        at,
        coarse_out,
        coarse_cot,
        scalars=True,
    )
    vd_y = swapped("gy", one, two)
    u_x = swapped("gx", *call(sides_kernel, [(2, ny + 4, k, nz)] * 2, [], 500_000_000, at, u, *u_y, scalars=True))
    inner, pre_in, wp, b_in = call(
        conv_inner_kernel,
        [(nx, 3 * k, (ny + 4) * nz), (nx - 2, h, (ny + 2) * nz), (3 * h, 27 * k), (h, 1)],
        [],
        2_500_000_000,
        at,
        u,
        *u_y,
        c_conv,
        coarse_bias_in[None, :],
        scalars=True,
    )
    vd_x = swapped("gx", *call(sides_kernel, [(1, ny + 2, 2 * k, nz)] * 2, [], 500_000_000, at, vd, *vd_y, scalars=True))
    outer, pre_out = call(
        conv_outer_kernel,
        [(4, 3 * k, (ny + 4) * nz), (4, h, (ny + 2) * nz)],
        [],
        4_000_000_000,
        at,
        inner,
        *u_x,
        wp,
        b_in,
        scalars=True,
    )
    q, c_gpre, low, coarse_grads = call(
        lambda *refs: coarse_kernel(factor, size_x, size_y, *refs),
        [(nx + 2, ny + 2, 2 * k, nz), (nx + 2, h, (ny + 2) * nz), (nx, k, ny * nz), (16 * k, 128)],
        [
            (nx, h, ny * nz),
            (nx, 2 * k, ny * nz),
            (9 * k + 16 + 2 * k, 4 * h),
            (9 * k + 2 * k, 4 * h),
            (2 * k, 128),
        ],
        6_000_000_000,
        at,
        inner,
        outer,
        pre_in,
        pre_out,
        vd,
        *vd_y,
        *vd_x,
        coarse_proj,
        coarse_bias_out[None, :],
        scalars=True,
    )
    coarse_grads = half_sum(coarse_grads, CORE)
    (dq,) = call(coarse_back_kernel, [(nx, ny, 2 * k, nz)], [], 2_500_000_000, c_gpre, low, cot_u, c_conv)
    coarse_grads, q, dq = tied(coarse_grads, q, dq)
    coarse_grads = quarter_sum(coarse_grads, X_NEAR, Y_NEAR)

    fx, fy = 2 * nx, 2 * ny
    field, cot, gpre, fine_grads = call(
        lambda *refs: fine_kernel(factor, *refs),
        [(fx, fy, 2 * fk, nz), (fx, fy, 2 * fk, nz), (fx, fy, fh, nz), (10 * fk, 128)],
        [
            (fx + 2, 3 * fk, (fy + 2) * nz),
            (fx, fk, fy * nz),
            (fx, 2 * fk, fy * nz),
            (9 * fk + 16 + 2 * fk, 4 * fh),
            (9 * fk + 2 * fk, 4 * fh),
            (2 * fk, 128),
        ],
        9_000_000_000,
        q,
        dq,
        f_conv,
        fine_bias_in[None, :],
        fine_proj,
        fine_bias_out[None, :],
    )
    coarse_grads, fine_grads = tied(coarse_grads, fine_grads)
    fine_grads = half_sum(fine_grads, CORE)

    sums = four_sum(coarse_grads, fine_grads, X_FAR, Y_FAR)
    *sums, gpre = four_sum(*sums, Z_ONE, Z_TWO, gpre)
    cot, columns, rows = call(
        fine_back_kernel,
        [cot.shape, (2, fx + 2, fk, nz), (2, fy, fk, nz)],
        [(fx + 4, fh, fy * nz)],
        4_000_000_000,
        gpre,
        cot,
        f_conv,
    )
    low, high = halos("gy", columns[0], columns[1])
    (field,) = call(channels_first_kernel, [(2 * fk, fx, fy, nz)], [], 1_000_000_000, field)
    rows, field = tied(rows, field)
    (rows,) = call(corners_kernel, [rows.shape], [], 6_000_000_000, rows, low, high)
    below, above = halos("gx", rows[0], rows[1])
    sums = pair_sum(*sums, Z_FAR)
    (cot,) = call(rims_kernel, [(2 * fk, fx, fy, nz)], [], 2_000_000_000, cot, low, high, below, above)
    coarse_grads, fine_grads = four_whole(*sums, X_NEAR, Y_NEAR)
    other = partner(jnp.concatenate([coarse_grads, fine_grads], axis=0), CORE)
    cut = coarse_grads.shape[0]
    sums = (coarse_grads, other[:cut], fine_grads, other[cut:])

    grads = call(
        unpack_kernel,
        [(27, fk, fh), (1, fh), (2 * fk, fh), (1, 2 * fk), (27, k, h), (1, h), (2 * k, h), (1, 2 * k)],
        [(16 * k, 128), (10 * fk, 128)],
        1_000_000,
        at,
        *sums,
        scalars=True,
    )
    f_conv, f_in, f_proj, f_out, c_conv, c_in, c_proj, c_out = grads
    return (
        field,
        cot,
        jnp.transpose(f_conv, (0, 2, 1)),
        f_in[0],
        f_proj,
        f_out[0],
        jnp.transpose(c_conv, (0, 2, 1)),
        c_in[0],
        c_proj,
        c_out[0],
    )


def solution(mesh):
    split_field = P(None, "gx", "gy", None)
    return jax.shard_map(
        local,
        mesh=mesh,
        in_specs=(split_field, split_field) + (P(),) * 8,
        out_specs=(split_field, split_field) + (P(),) * 8,
        check_vma=False,
    )
```
